512 devices in a mesh: dp: 512 (over y, z, x, core).
Axes of the slice: x: 4, y: 8, z: 8, core: 2. Of those that a mesh axis runs over, the one named last changes fastest.
Arguments:
- features: bfloat16 [65536, 1024], P('dp')
- head_rows: bfloat16 [1024, 1024], P('dp')
- poses: bfloat16 [65536, 1024], P('dp')
- match_ids: int32 [65536], replicated, may hold values from 0 to 65535, as said below
- logit_scale: float32 [1], replicated, may hold values from 5 to 10
- logit_bias: float32 [1], replicated, may hold values from -4 to -2
Outputs:
- pose_grad: bfloat16 [65536, 1024], P('dp')
- head_grad: float32 [1024, 1024], P('dp')
- loss_terms: float32 [2], replicated
- scale_grad: float32 [1], replicated
The draws below stay inside these ranges and needn't reach their ends.
Inputs may be any that keep to these rules, and one draw needn't show every extreme that they name: `match_ids`: samples with equal ids are positive pairs; every sample matches itself.
All inputs are finite; a program needn't handle non-finite values.
Results may differ from the reference program's by a relative error of at most 0.006.
Values may be sent and summed in bfloat16 or wider, within the bound.
A program may use at most 64 MiB of HBM per device.

```python
import math
import jax
import jax.numpy as jnp
from jax import lax

F = 1024
D = 1024
ROWS = 128
REACH = 2
BATCH = 65536
N_DP = 512


def shared_image(key):
    key_feat = jax.random.fold_in(key, 11)
    key_head = jax.random.fold_in(key, 13)
    features = jax.random.normal(key_feat, (BATCH, F), jnp.float32)
    head_table = jax.random.normal(key_head, (F, D), jnp.float32) * F ** (-0.5)
    return (features, head_table)


def draw_features(key, part):
    features, head_table = shared_image(key)
    return features.astype(jnp.bfloat16)


def draw_head_rows(key, part):
    features, head_table = shared_image(key)
    return head_table.astype(jnp.bfloat16)


def draw_match_ids(key, part):
    key = jax.random.fold_in(key, 5)
    position = jnp.arange(BATCH, dtype=jnp.int32)
    level = 1 + 8 * position // BATCH
    jitter = jax.random.randint(key, (BATCH,), 0, 8, dtype=jnp.int32) % level
    anchor = jnp.minimum(position + jitter, BATCH - 1)
    group_id = anchor // level * level
    return jnp.where(position == BATCH - 1, BATCH - 1, group_id).astype(jnp.int32)


def draw_poses(key, part):
    features, head_table = shared_image(key)
    proj = jnp.dot(features, head_table, precision=lax.Precision.HIGHEST)
    key = jax.random.fold_in(key, 7)
    key_rows = jax.random.fold_in(key, 0)
    key_cols = jax.random.fold_in(key, 1)
    key_base = jax.random.fold_in(key, 2)
    key_align = jax.random.fold_in(key, 4)
    row_scale = jnp.exp(jax.random.uniform(key_rows, (BATCH, 1), jnp.float32, 0.0, math.log(10.0)))
    col_scale = jnp.exp(jax.random.uniform(key_cols, (1, D), jnp.float32, 0.0, math.log(10.0)))
    base = jax.random.normal(key_base, (BATCH, D), jnp.float32)
    strength = jax.random.uniform(key_align, (BATCH // ROWS, 1), jnp.float32, 0.0, 3.0)
    strength = jnp.repeat(strength, ROWS, axis=0)
    noise = col_scale * base
    aligned = 4.6 * strength * proj
    return (0.002 * row_scale * (noise + aligned)).astype(jnp.bfloat16)


def setup_inputs(seed: int = 0) -> dict:
    key_list = jax.random.split(jax.random.key(seed), 7)
    features = draw_features(jax.random.fold_in(key_list[6], 71), 0)
    head_rows = draw_head_rows(jax.random.fold_in(key_list[6], 71), 0)
    poses = draw_poses(jax.random.fold_in(key_list[6], 71), 0)
    match_ids = draw_match_ids(jax.random.fold_in(key_list[6], 71), 0)
    logit_scale = jnp.clip(jax.random.uniform(key_list[4], (1,), jnp.float32, 5.0, 10.0), 5.0, 10.0)
    logit_bias = jnp.clip(jax.random.uniform(key_list[5], (1,), jnp.float32, -4.0, -2.0), -4.0, -2.0)
    return {"features": features, "head_rows": head_rows, "poses": poses, "match_ids": match_ids, "logit_scale": logit_scale, "logit_bias": logit_bias}


EPS = 1e-06

def tile_terms(left_emb, left_ids, right_emb, right_ids, scale_val, bias_val):
    inner = lax.dot_general(left_emb, right_emb, (((1,), (1,)), ((), ())), preferred_element_type=jnp.float32)
    logits = scale_val * inner + bias_val
    matched = left_ids[:, None] == right_ids[None, :]
    sign_table = jnp.where(matched, jnp.float32(1.0), jnp.float32(-1.0))
    loss_sum = -jnp.sum(jax.nn.log_sigmoid(sign_table * logits))
    gradient = jax.nn.sigmoid(logits) - matched.astype(jnp.float32)
    weight = (scale_val * gradient).astype(jnp.bfloat16)
    totals = jnp.stack([loss_sum, jnp.sum(gradient), jnp.sum(gradient * inner)])
    return (weight, totals)

def reference(features, head_rows, poses, match_ids, logit_scale, logit_bias):
    proj = jnp.dot(features, head_rows, preferred_element_type=jnp.float32)
    norm_img = jnp.sqrt(lax.optimization_barrier(jnp.sum(proj * proj, axis=1, keepdims=True)) + EPS)
    unit_img = proj / norm_img
    image_emb = unit_img.astype(jnp.bfloat16)
    pose_float = poses.astype(jnp.float32)
    norm_pose = jnp.sqrt(lax.optimization_barrier(jnp.sum(pose_float * pose_float, axis=1, keepdims=True)) + EPS)
    unit_pose = pose_float / norm_pose
    pose_emb = unit_pose.astype(jnp.bfloat16)
    scale_val = logit_scale[0]
    bias_val = logit_bias[0]
    img_blocks = image_emb.reshape(N_DP, ROWS, D)
    pose_blocks = pose_emb.reshape(N_DP, ROWS, D)
    id_blocks = match_ids.reshape(N_DP, ROWS)

    def visit(carried, position):
        pose_acc, totals = carried
        left_emb = lax.dynamic_index_in_dim(img_blocks, position, 0, keepdims=False)
        left_ids = lax.dynamic_index_in_dim(id_blocks, position, 0, keepdims=False)
        grad_left = jnp.zeros((ROWS, D), jnp.float32)
        for offset in range(-REACH, REACH + 1):
            partner = ((position + offset) % N_DP).astype(jnp.int32)
            right_emb = lax.dynamic_index_in_dim(pose_blocks, partner, 0, keepdims=False)
            right_ids = lax.dynamic_index_in_dim(id_blocks, partner, 0, keepdims=False)
            weight, partial_value = tile_terms(left_emb, left_ids, right_emb, right_ids, scale_val, bias_val)
            totals = totals + partial_value
            grad_left = grad_left + jnp.dot(weight, right_emb, preferred_element_type=jnp.float32)
            pose_term = lax.dot_general(weight, left_emb, (((0,), (0,)), ((), ())), preferred_element_type=jnp.float32)
            previous = lax.dynamic_index_in_dim(pose_acc, partner, 0, keepdims=False)
            pose_acc = lax.dynamic_update_index_in_dim(pose_acc, previous + pose_term, partner, 0)
        return ((pose_acc, totals), grad_left)
    start = (jnp.zeros((N_DP, ROWS, D), jnp.float32), jnp.zeros((3,), jnp.float32))
    (pose_acc, totals), grad_img = lax.scan(visit, start, jnp.arange(N_DP, dtype=jnp.int32))
    grad_img = grad_img.reshape(BATCH, D)
    along_img = lax.optimization_barrier(jnp.sum(unit_img * grad_img, axis=1, keepdims=True))
    grad_proj = ((grad_img - unit_img * along_img) / norm_img).astype(jnp.bfloat16)
    head_grad = lax.dot_general(features, grad_proj, (((0,), (0,)), ((), ())), preferred_element_type=jnp.float32)
    grad_pose = pose_acc.reshape(BATCH, D)
    along_pose = lax.optimization_barrier(jnp.sum(unit_pose * grad_pose, axis=1, keepdims=True))
    pose_grad = ((grad_pose - unit_pose * along_pose) / norm_pose).astype(jnp.bfloat16)
    loss_terms = totals[:2] / BATCH
    scale_grad = totals[2:] / BATCH
    return (pose_grad, head_grad, loss_terms, scale_grad)
```

```python
import functools

import jax
import jax.numpy as jnp
from jax import lax
from jax.experimental import pallas as pl
from jax.experimental.pallas import tpu as pltpu
from jax.sharding import PartitionSpec as P

REACH = 2
WINDOW = 2 * REACH + 1
EPS = 1e-06
ROWS = 128
COLS = 128
GROUP = 8
SIDE = 8
CELLS = SIDE * SIDE
COUNT = GROUP * CELLS
BATCH = ROWS * COUNT
WIDTH = GROUP * COLS
TILE = 16
HALF = ROWS // 2

F32 = jnp.float32
BF16 = jnp.bfloat16


def remote(src, dst, send_sem, recv_sem, device):
    return pltpu.make_async_remote_copy(
        src_ref=src,
        dst_ref=dst,
        send_sem=send_sem,
        recv_sem=recv_sem,
        device_id=(device,),
        device_id_type=pl.DeviceIdType.MESH,
    )


def dot(left, right, dims):
    return lax.dot_general(left, right, (dims, ((), ())), preferred_element_type=F32)


def softplus_parts(logits):
    tail = jnp.exp(-jnp.abs(logits))
    share = 1.0 / (1.0 + tail)
    sigmoid = jnp.where(logits >= 0, share, tail * share)
    return jnp.log1p(tail), sigmoid


def kernel(
    feat_hbm, head_ref, pose_hbm, ids_ref, scale_ref, bias_ref,
    pose_grad_ref, head_grad_ref, loss_ref, scale_grad_ref,
    feats, feats_t, pose_raw, poses, embs, piece_src, piece, tile_f32, head,
    proj_src, proj, unit, inv_pose, gp_src, gp, part_src, part, fin_src, fin,
    tot_src, tot_group, tot_z_src, tot_z, tot_y_src, tot_y,
    local_sem, piece_s, piece_r, feat_s, feat_r, head_s, head_r, pose_s, pose_r, emb_s, emb_r,
    proj_s, proj_r, gp_s, gp_r, part_s, part_r, fin_s, fin_r, tot_s, tot_r,
):
    me = lax.axis_index("dp")
    slot = lax.rem(me, GROUP)
    cell = me // GROUP
    y = cell // SIDE
    z = lax.rem(cell, SIDE)
    core = lax.rem(me, 2)
    base = me - slot
    sibling = me + 1 - 2 * core

    def mate_slot(step):
        return lax.rem(slot + step, GROUP)

    def plane_cell(step_y, step_z):
        return lax.rem(y + step_y, SIDE) * SIDE + lax.rem(z + step_z, SIDE)

    def ring(step):
        return lax.rem(me + step + COUNT, COUNT)

    load_feat = pltpu.make_async_copy(feat_hbm, feats.at[slot], local_sem.at[0])
    load_pose = pltpu.make_async_copy(pose_hbm, pose_raw, local_sem.at[1])
    load_pose.start()
    load_feat.start()

    barrier = pltpu.get_barrier_semaphore()

    def greet(device):
        pl.semaphore_signal(barrier, inc=1, device_id=(device,), device_id_type=pl.DeviceIdType.MESH)

    for step in range(1, GROUP):
        greet(base + mate_slot(step))
    for step in (-2, -1, 1, 2):
        greet(ring(step))

    @pl.loop(1, CELLS)
    def _(step):
        greet(plane_cell(step // SIDE, lax.rem(step, SIDE)) * GROUP + slot)

    rows = head_ref[...].astype(F32)
    piece_src[...] = jnp.zeros_like(piece_src)
    for number in range(GROUP):
        piece_src[number, 0:2, :] = rows[:, number * COLS : (number + 1) * COLS]
    piece[slot] = piece_src[slot]

    pl.semaphore_wait(barrier, GROUP - 1 + 4 + CELLS - 1)

    piece_copies = []
    for step in (4, 5, 3, 2, 6, 7, 1):
        copy = remote(
            piece_src.at[mate_slot(step)], piece.at[slot], piece_s.at[step], piece_r.at[step], base + mate_slot(step)
        )
        copy.start()
        piece_copies.append(copy)

    load_feat.wait()
    right = base + mate_slot(2)
    left = base + mate_slot(6)

    def half(of_slot, number):
        return feats.at[of_slot, pl.ds(number * HALF, HALF), :]

    def send_half(of_slot, number, device, sem):
        copy = remote(half(of_slot, number), half(of_slot, number), feat_s.at[sem], feat_r.at[sem], device)
        copy.start()
        return copy

    def send_block(of_slot, sem):
        copy = remote(feats.at[of_slot], feats.at[of_slot], feat_s.at[sem], feat_r.at[sem], sibling)
        copy.start()
        return copy

    right_a = send_half(slot, 0, right, 0)
    left_b = send_half(slot, 1, left, 1)
    right_b = send_half(slot, 1, right, 2)
    left_a = send_half(slot, 0, left, 3)
    block_own = send_block(slot, 6)

    for copy in piece_copies:
        copy.wait_recv()
    for number in range(GROUP):
        tile_f32[2 * number : 2 * number + 2, :] = piece[number, 0:2, :]
    head[cell] = tile_f32[...].astype(BF16)

    @pl.loop(1, CELLS)
    def _(step):
        device = plane_cell(step // SIDE, lax.rem(step, SIDE)) * GROUP + slot
        remote(head.at[cell], head.at[cell], head_s, head_r, device).start()

    load_pose.wait()
    raw = pose_raw[...].astype(F32)
    inv_p = 1.0 / jnp.sqrt(jnp.sum(raw * raw, axis=1, keepdims=True) + EPS)
    inv_pose[...] = jnp.broadcast_to(inv_p, (ROWS, COLS))
    poses[REACH] = (raw * inv_p).astype(BF16)

    right_a.wait_recv()
    right_a2 = send_half(mate_slot(6), 0, right, 4)
    left_b.wait_recv()
    left_b2 = send_half(mate_slot(2), 1, left, 5)
    right_b.wait_recv()
    block_left = send_block(mate_slot(6), 7)
    left_a.wait_recv()
    block_right = send_block(mate_slot(2), 8)
    right_a2.wait_recv()
    left_b2.wait_recv()
    block_far = send_block(mate_slot(4), 9)

    def exchange(blocks, sems, semr):
        ahead = remote(blocks.at[REACH], blocks.at[0], sems.at[0], semr.at[0], ring(2))
        behind = remote(blocks.at[REACH], blocks.at[4], sems.at[1], semr.at[4], ring(-2))
        beside = remote(
            blocks.at[REACH], blocks.at[1 + 2 * core], sems.at[2], semr.at[1 + 2 * core], sibling
        )
        passed = remote(
            blocks.at[4 - 4 * core], blocks.at[3 - 2 * core], sems.at[3], semr.at[3 - 2 * core], sibling
        )
        ahead.start()
        behind.start()
        beside.start()

        def forward():
            ahead.wait_recv()
            behind.wait_recv()
            passed.start()

        def finish():
            remote(blocks.at[REACH], blocks.at[1], sems.at[2], semr.at[1], sibling).wait_recv()
            remote(blocks.at[REACH], blocks.at[3], sems.at[3], semr.at[3], sibling).wait_recv()

        def drain():
            ahead.wait_send()
            behind.wait_send()
            beside.wait_send()
            passed.wait_send()

        return forward, finish, drain

    pose_forward, pose_finish, pose_drain = exchange(poses, pose_s, pose_r)

    for copy in (block_own, block_left, block_right, block_far):
        copy.wait_recv()
    for number in range(GROUP):
        feats_t[:, number * ROWS : (number + 1) * ROWS] = feats[number].T

    pltpu.make_async_copy(head.at[pl.ds(0, CELLS - 1)], head.at[pl.ds(0, CELLS - 1)], head_r).wait()
    head_cols = head[...].reshape(WIDTH, COLS)
    proj_copies = []
    for step in (4, 5, 3, 2, 6, 7, 1):
        to = mate_slot(step)
        proj_src[step] = dot(feats[to], head_cols, ((1,), (0,)))
        copy = remote(proj_src.at[step], proj.at[slot], proj_s.at[step], proj_r.at[step], base + to)
        copy.start()
        proj_copies.append(copy)
    proj[slot] = dot(feats[slot], head_cols, ((1,), (0,)))

    pose_forward()
    pose_finish()
    for copy in proj_copies:
        copy.wait_recv()

    square = jnp.zeros((ROWS, COLS), F32)
    for number in range(GROUP):
        value = proj[number]
        square = square + value * value
    inv_i = 1.0 / jnp.sqrt(jnp.sum(square, axis=1, keepdims=True) + EPS)
    for number in range(GROUP):
        value = proj[number] * inv_i
        unit[:, number * COLS : (number + 1) * COLS] = value
        embs[REACH, :, number * COLS : (number + 1) * COLS] = value.astype(BF16)

    scale = scale_ref[0]
    bias = bias_ref[0]

    def ids_of(step):
        return ids_ref[pl.ds(ring(step), 1), :]

    own_ids = jnp.broadcast_to(ids_of(0), (ROWS, ROWS)).T

    def window_terms(left_emb, blocks, with_totals):
        weights = []
        totals = [jnp.zeros((1, COLS), F32) for _ in range(3)]
        for number in range(WINDOW):
            inner = dot(left_emb, blocks[number], ((1,), (1,)))
            logits = scale * inner + bias
            matched = own_ids == ids_of(number - REACH)
            tail, sigmoid = softplus_parts(logits)
            gradient = sigmoid - matched.astype(F32)
            weights.append((scale * gradient).astype(BF16))
            if with_totals:
                signed = jnp.where(matched, logits, -logits)
                loss = tail - jnp.minimum(signed, 0.0)
                for place, term in enumerate((loss, gradient, gradient * inner)):
                    totals[place] = totals[place] + jnp.sum(term, axis=0, keepdims=True)
        return jnp.concatenate(weights, axis=1), totals

    weight, totals = window_terms(embs[REACH], poses, True)
    tot_src[...] = jnp.zeros_like(tot_src)
    for place in range(3):
        tot_src[place : place + 1, :] = totals[place]
    tot_copies = []
    for step in range(1, GROUP):
        copy = remote(tot_src, tot_group.at[slot], tot_s.at[step], tot_r.at[step], base + mate_slot(step))
        copy.start()
        tot_copies.append(copy)
    tot_group[slot] = tot_src[...]

    grad_img = dot(weight, poses[...].reshape(WINDOW * ROWS, WIDTH), ((1,), (0,)))
    unit_img = unit[...]
    along = jnp.sum(unit_img * grad_img, axis=1, keepdims=True)
    grad_proj = ((grad_img - unit_img * along) * inv_i).astype(BF16)
    for number in range(GROUP):
        gp_src[number] = grad_proj[:, number * COLS : (number + 1) * COLS]
    gp_copies = []
    for step in (4, 5, 3, 2, 6, 7, 1):
        to = mate_slot(step)
        copy = remote(gp_src.at[to], gp.at[slot], gp_s.at[step], gp_r.at[step], base + to)
        copy.start()
        gp_copies.append(copy)
    gp[slot] = gp_src[slot]

    for copy in tot_copies:
        copy.wait_recv()
    group_sum = tot_group[0]
    for number in range(1, GROUP):
        group_sum = group_sum + tot_group[number]
    tot_z_src[...] = group_sum
    tot_z[z] = group_sum
    z_copies = []
    for step in range(1, SIDE):
        copy = remote(
            tot_z_src, tot_z.at[z], tot_s.at[8 + step], tot_r.at[8 + step], plane_cell(0, step) * GROUP + slot
        )
        copy.start()
        z_copies.append(copy)

    for copy in gp_copies:
        copy.wait_recv()

    @pl.loop(0, SIDE)
    def _(step_y):
        row = lax.rem(y + step_y, SIDE)
        start = pl.multiple_of(row * (SIDE * TILE), SIDE * TILE)
        value = dot(feats_t[pl.ds(start, SIDE * TILE), :], gp[...].reshape(GROUP * ROWS, COLS), ((1,), (0,)))
        part_src[pl.ds(row * SIDE, SIDE)] = value.astype(BF16).reshape(SIDE, TILE, COLS)

        @pl.loop(0, SIDE)
        def _(step_z):
            to = plane_cell(step_y, step_z)

            @pl.when(step_y + step_z > 0)
            def _():
                remote(part_src.at[to], part.at[cell], part_s, part_r, to * GROUP + slot).start()

    part[cell] = part_src[cell]

    emb_forward, emb_finish, emb_drain = exchange(embs, emb_s, emb_r)

    for copy in z_copies:
        copy.wait_recv()
    z_sum = tot_z[0]
    for number in range(1, SIDE):
        z_sum = z_sum + tot_z[number]
    tot_y_src[...] = z_sum
    tot_y[y] = z_sum
    y_copies = []
    for step in range(1, SIDE):
        copy = remote(
            tot_y_src, tot_y.at[y], tot_s.at[16 + step], tot_r.at[16 + step], plane_cell(step, 0) * GROUP + slot
        )
        copy.start()
        y_copies.append(copy)

    emb_forward()
    emb_finish()
    pose_weight, _ = window_terms(poses[REACH], embs, False)
    grad_pose = dot(pose_weight, embs[...].reshape(WINDOW * ROWS, WIDTH), ((1,), (0,)))
    inv_q = inv_pose[:, 0:1]
    unit_pose = pose_raw[...].astype(F32) * inv_q
    along_pose = jnp.sum(unit_pose * grad_pose, axis=1, keepdims=True)
    pose_grad_ref[...] = ((grad_pose - unit_pose * along_pose) * inv_q).astype(BF16)

    pltpu.make_async_copy(part.at[pl.ds(0, CELLS - 1)], part.at[pl.ds(0, CELLS - 1)], part_r).wait()
    summed = jnp.sum(part[...].astype(F32), axis=0)
    fin_src[...] = jnp.zeros_like(fin_src)
    for number in range(GROUP):
        fin_src[number, 0:2, :] = summed[2 * number : 2 * number + 2, :]
    fin_copies = []
    for step in (4, 5, 3, 2, 6, 7, 1):
        to = mate_slot(step)
        copy = remote(fin_src.at[to], fin.at[slot], fin_s.at[step], fin_r.at[step], base + to)
        copy.start()
        fin_copies.append(copy)
    fin[slot] = fin_src[slot]

    for copy in y_copies:
        copy.wait_recv()
    y_sum = tot_y[0]
    for number in range(1, SIDE):
        y_sum = y_sum + tot_y[number]
    y_sum = y_sum / BATCH
    loss_ref[0] = jnp.sum(y_sum[0:1, :])
    loss_ref[1] = jnp.sum(y_sum[1:2, :])
    scale_grad_ref[0] = jnp.sum(y_sum[2:3, :])

    for copy in fin_copies:
        copy.wait_recv()
    for number in range(GROUP):
        head_grad_ref[:, number * COLS : (number + 1) * COLS] = fin[number, 0:2, :]

    for copy in piece_copies + proj_copies + gp_copies + fin_copies + tot_copies + z_copies + y_copies:
        copy.wait_send()
    for copy in (right_a, left_b, right_b, left_a, right_a2, left_b2, block_own, block_left, block_right, block_far):
        copy.wait_send()
    pose_drain()
    emb_drain()
    pltpu.make_async_copy(head.at[pl.ds(0, CELLS - 1)], head.at[pl.ds(0, CELLS - 1)], head_s).wait()
    pltpu.make_async_copy(part_src.at[pl.ds(0, CELLS - 1)], part_src.at[pl.ds(0, CELLS - 1)], part_s).wait()


def local(features, head_rows, poses, match_ids, logit_scale, logit_bias):
    vmem = pl.BlockSpec(memory_space=pltpu.VMEM)
    smem = pl.BlockSpec(memory_space=pltpu.SMEM)
    hbm = pl.BlockSpec(memory_space=pl.ANY)
    dma = pltpu.SemaphoreType.DMA
    block = (ROWS, WIDTH)
    square = (GROUP, ROWS, COLS)
    return pl.pallas_call(
        kernel,
        name="contrastive",
        out_shape=(
            jax.ShapeDtypeStruct(block, BF16),
            jax.ShapeDtypeStruct((2, WIDTH), F32),
            jax.ShapeDtypeStruct((2,), F32),
            jax.ShapeDtypeStruct((1,), F32),
        ),
        in_specs=[hbm, vmem, hbm, vmem, smem, smem],
        out_specs=(vmem, vmem, smem, smem),
        scratch_shapes=[
            pltpu.VMEM((GROUP,) + block, BF16),
            pltpu.VMEM((WIDTH, GROUP * ROWS), BF16),
            pltpu.VMEM(block, BF16),
            pltpu.VMEM((WINDOW,) + block, BF16),
            pltpu.VMEM((WINDOW,) + block, BF16),
            pltpu.VMEM((GROUP, 8, COLS), F32),
            pltpu.VMEM((GROUP, 8, COLS), F32),
            pltpu.VMEM((TILE, COLS), F32),
            pltpu.VMEM((CELLS, TILE, COLS), BF16),
            pltpu.VMEM(square, F32),
            pltpu.VMEM(square, F32),
            pltpu.VMEM(block, F32),
            pltpu.VMEM((ROWS, COLS), F32),
            pltpu.VMEM(square, BF16),
            pltpu.VMEM(square, BF16),
            pltpu.VMEM((CELLS, TILE, COLS), BF16),
            pltpu.VMEM((CELLS, TILE, COLS), BF16),
            pltpu.VMEM((GROUP, 8, COLS), F32),
            pltpu.VMEM((GROUP, 8, COLS), F32),
            pltpu.VMEM((8, COLS), F32),
            pltpu.VMEM((GROUP, 8, COLS), F32),
            pltpu.VMEM((8, COLS), F32),
            pltpu.VMEM((SIDE, 8, COLS), F32),
            pltpu.VMEM((8, COLS), F32),
            pltpu.VMEM((SIDE, 8, COLS), F32),
            dma((2,)),
            dma((GROUP,)), dma((GROUP,)),
            dma((10,)), dma((10,)),
            dma, dma,
            dma((4,)), dma((WINDOW,)),
            dma((4,)), dma((WINDOW,)),
            dma((GROUP,)), dma((GROUP,)),
            dma((GROUP,)), dma((GROUP,)),
            dma, dma,
            dma((GROUP,)), dma((GROUP,)),
            dma((24,)), dma((24,)),
        ],
        compiler_params=pltpu.CompilerParams(
            collective_id=0, has_side_effects=True, vmem_limit_bytes=48 * 1024 * 1024
        ),
    )(features, head_rows, poses, match_ids.reshape(COUNT, ROWS), logit_scale, logit_bias)


def solution(mesh):
    return jax.shard_map(
        local,
        mesh=mesh,
        in_specs=(P("dp", None), P("dp", None), P("dp", None), P(), P(), P()),
        out_specs=(P("dp", None), P("dp", None), P(), P()),
        check_vma=False,
    )
```

```python
import jax
import jax.numpy as jnp
from jax import lax
from jax.experimental import pallas as pl
from jax.experimental.pallas import tpu as pltpu
from jax.sharding import PartitionSpec as P

REACH = 2
WINDOW = 2 * REACH + 1
EPS = 1e-06
ROWS = 128
COLS = 128
GROUP = 8
SIDE = 8
CELLS = SIDE * SIDE
COUNT = GROUP * CELLS
BATCH = ROWS * COUNT
WIDTH = GROUP * COLS
TILE = 16
HALF = ROWS // 2
FAR_FIRST = (4, 5, 3, 2, 6, 7, 1)
SIDE_FAR_FIRST = (4, 3, 5, 2, 6, 1, 7)
PLANE = [(down, over) for down in SIDE_FAR_FIRST + (0,) for over in SIDE_FAR_FIRST + (0,) if down or over]

F32 = jnp.float32
BF16 = jnp.bfloat16


def remote(src, dst, send_sem, recv_sem, device):
    return pltpu.make_async_remote_copy(
        src_ref=src,
        dst_ref=dst,
        send_sem=send_sem,
        recv_sem=recv_sem,
        device_id=(device,),
        device_id_type=pl.DeviceIdType.MESH,
    )


def dot(left, right, dims):
    return lax.dot_general(left, right, (dims, ((), ())), preferred_element_type=F32)


def softplus_parts(logits):
    tail = jnp.exp(-jnp.abs(logits))
    share = 1.0 / (1.0 + tail)
    sigmoid = jnp.where(logits >= 0, share, tail * share)
    return jnp.log1p(tail), sigmoid


def kernel(
    feat_hbm, head_hbm, pose_hbm, ids_hbm, scale_ref, bias_ref,
    pose_grad_hbm, head_grad_ref, loss_ref, scale_grad_ref,
    feats, feats_t, pose_raw, poses, embs, pose_held, emb_held, pose_out, ids, head_rows, piece_src, piece, tile_f32, head,
    proj_src, proj, unit, inv_pose, gp_src, gp, part_src, part, fin_src, fin,
    tot_src, tot_group, tot_z_src, tot_z, tot_y_src, tot_y,
    local_sem, piece_s, piece_r, feat_s, feat_r, head_s, head_r, pose_s, pose_r, emb_s, emb_r,
    proj_s, proj_r, gp_s, gp_r, part_s, part_r, fin_s, fin_r, tot_s, tot_r,
):
    me = lax.axis_index("dp")
    slot = lax.rem(me, GROUP)
    cell = me // GROUP
    y = cell // SIDE
    z = lax.rem(cell, SIDE)
    core = lax.rem(me, 2)
    base = me - slot
    sibling = me + 1 - 2 * core
    lines = [lax.rem(y + step, SIDE) * SIDE for step in range(SIDE)]
    spots = [lax.rem(z + step, SIDE) for step in range(SIDE)]

    def mate_slot(step):
        return lax.rem(slot + step, GROUP)

    def turned(place, step):
        return lax.rem(place + step, SIDE)

    def at(of_y, of_z):
        return (of_y * SIDE + of_z) * GROUP + slot

    def ring(step):
        return lax.rem(me + step + COUNT, COUNT)

    loads = [
        pltpu.make_async_copy(source, target, local_sem.at[number])
        for number, (source, target) in enumerate((
            (head_hbm, head_rows),
            (feat_hbm, feats.at[slot]),
            (pose_hbm, pose_raw),
            (ids_hbm, ids),
        ))
    ]
    load_head, load_feat, load_pose, load_ids = loads
    for load in loads:
        load.start()

    barrier = pltpu.get_barrier_semaphore()

    def greet(device):
        pl.semaphore_signal(barrier, inc=1, device_id=(device,), device_id_type=pl.DeviceIdType.MESH)

    for step in FAR_FIRST:
        greet(base + mate_slot(step))
    for down, over in PLANE:
        greet((lines[down] + spots[over]) * GROUP + slot)

    load_head.wait()
    rows = head_rows[...].astype(F32)
    piece_src[...] = jnp.zeros_like(piece_src)
    for number in range(GROUP):
        piece_src[number, 0:2, :] = rows[:, number * COLS : (number + 1) * COLS]
    piece[slot] = piece_src[slot]

    pl.semaphore_wait(barrier, GROUP - 1 + CELLS - 1)

    def exchange(blocks, held, sems, semr):
        own = blocks.at[REACH]
        ahead = remote(own, blocks.at[0], sems.at[0], semr.at[0], ring(2))
        behind = remote(own, blocks.at[4], sems.at[1], semr.at[4], ring(-2))
        ahead_cell = remote(own, held, sems.at[0], semr.at[2], ring(GROUP))
        behind_cell = remote(own, held, sems.at[1], semr.at[2], ring(-GROUP))
        ahead_relay = remote(held, blocks.at[0], sems.at[4], semr.at[0], base + core)
        behind_relay = remote(held, blocks.at[4], sems.at[4], semr.at[4], base + GROUP - 2 + core)
        beside = remote(own, blocks.at[1 + 2 * core], sems.at[2], semr.at[1 + 2 * core], sibling)
        passed = remote(
            blocks.at[4 - 4 * core], blocks.at[3 - 2 * core], sems.at[3], semr.at[3 - 2 * core], sibling
        )

        def to_cells():
            pl.when(slot >= GROUP - 2)(ahead_cell.start)
            pl.when(slot < 2)(behind_cell.start)

        def direct():
            pl.when(slot < GROUP - 2)(ahead.start)
            pl.when(slot >= 2)(behind.start)
            beside.start()

        def relay():
            @pl.when(slot >= GROUP - 2)
            def _():
                ahead_cell.wait_recv()
                ahead_relay.start()

            @pl.when(slot < 2)
            def _():
                behind_cell.wait_recv()
                behind_relay.start()

        def forward():
            ahead.wait_recv()
            behind.wait_recv()
            passed.start()

        def finish():
            remote(own, blocks.at[1], sems.at[2], semr.at[1], sibling).wait_recv()
            remote(own, blocks.at[3], sems.at[3], semr.at[3], sibling).wait_recv()

        def drain():
            ahead.wait_send()
            behind.wait_send()
            beside.wait_send()
            passed.wait_send()
            pl.when(slot >= GROUP - 2)(ahead_relay.wait_send)
            pl.when(slot < 2)(behind_relay.wait_send)

        return to_cells, direct, relay, forward, finish, drain

    pose_to_cells, pose_direct, pose_relay, pose_forward, pose_finish, pose_drain = exchange(
        poses, pose_held, pose_s, pose_r
    )
    emb_to_cells, emb_direct, emb_relay, emb_forward, emb_finish, emb_drain = exchange(embs, emb_held, emb_s, emb_r)

    piece_copies = []
    for step in FAR_FIRST:
        to = mate_slot(step)
        copy = remote(piece_src.at[to], piece.at[slot], piece_s.at[step], piece_r.at[step], base + to)
        copy.start()
        piece_copies.append(copy)

    load_feat.wait()
    right = base + mate_slot(2)
    left = base + mate_slot(6)

    def half(of_slot, number):
        return feats.at[of_slot, pl.ds(number * HALF, HALF), :]

    def send_half(of_slot, number, device, sem):
        copy = remote(half(of_slot, number), half(of_slot, number), feat_s.at[sem], feat_r.at[sem], device)
        copy.start()
        return copy

    def send_block(of_slot, sem):
        copy = remote(feats.at[of_slot], feats.at[of_slot], feat_s.at[sem], feat_r.at[sem], sibling)
        copy.start()
        return copy

    right_a = send_half(slot, 0, right, 0)
    left_b = send_half(slot, 1, left, 1)
    right_b = send_half(slot, 1, right, 2)
    left_a = send_half(slot, 0, left, 3)
    block_own = send_block(slot, 6)

    load_pose.wait()
    raw = pose_raw[...].astype(F32)
    inv_p = 1.0 / jnp.sqrt(jnp.sum(raw * raw, axis=1, keepdims=True) + EPS)
    inv_pose[...] = jnp.broadcast_to(inv_p, (ROWS, COLS))
    poses[REACH] = (raw * inv_p).astype(BF16)
    pose_to_cells()

    for copy in piece_copies:
        copy.wait_recv()
    for number in range(GROUP):
        tile_f32[2 * number : 2 * number + 2, :] = piece[number, 0:2, :]
    head[cell] = tile_f32[...].astype(BF16)
    for down, over in PLANE:
        device = (lines[down] + spots[over]) * GROUP + slot
        remote(head.at[cell], head.at[cell], head_s, head_r, device).start()

    right_a.wait_recv()
    right_a2 = send_half(mate_slot(6), 0, right, 4)
    left_b.wait_recv()
    left_b2 = send_half(mate_slot(2), 1, left, 5)

    pose_direct()
    pose_relay()

    right_b.wait_recv()
    block_left = send_block(mate_slot(6), 7)
    left_a.wait_recv()
    block_right = send_block(mate_slot(2), 8)
    right_a2.wait_recv()
    left_b2.wait_recv()
    block_far = send_block(mate_slot(4), 9)

    pltpu.make_async_copy(head.at[pl.ds(0, CELLS - 1)], head.at[pl.ds(0, CELLS - 1)], head_r).wait()
    for copy in (block_own, block_left, block_right, block_far):
        copy.wait_recv()
    proj_copies = []
    for step in FAR_FIRST:
        to = mate_slot(step)
        proj_src[step] = dot(feats[to], head[...].reshape(WIDTH, COLS), ((1,), (0,)))
        copy = remote(proj_src.at[step], proj.at[slot], proj_s.at[step], proj_r.at[step], base + to)
        copy.start()
        proj_copies.append(copy)
    proj[slot] = dot(feats[slot], head[...].reshape(WIDTH, COLS), ((1,), (0,)))

    pose_forward()
    for number in range(GROUP):
        feats_t[:, number * ROWS : (number + 1) * ROWS] = feats[number].T
    load_ids.wait()
    pose_finish()
    for copy in proj_copies:
        copy.wait_recv()

    square = jnp.zeros((ROWS, COLS), F32)
    for number in range(GROUP):
        value = proj[number]
        square = square + value * value
    inv_i = 1.0 / jnp.sqrt(jnp.sum(square, axis=1, keepdims=True) + EPS)
    for number in range(GROUP):
        value = proj[number] * inv_i
        unit[:, number * COLS : (number + 1) * COLS] = value
        embs[REACH, :, number * COLS : (number + 1) * COLS] = value.astype(BF16)
    emb_to_cells()

    scale = jnp.broadcast_to(scale_ref[...], (ROWS, ROWS))
    bias = jnp.broadcast_to(bias_ref[...], (ROWS, ROWS))

    def ids_of(step):
        return ids[pl.ds(ring(step), 1), :]

    own_ids = jnp.broadcast_to(ids_of(0), (ROWS, ROWS)).T

    def window_terms(left_emb, blocks, with_totals):
        weights = []
        totals = [jnp.zeros((1, COLS), F32) for _ in range(3)]
        for number in range(WINDOW):
            inner = dot(left_emb, blocks[number], ((1,), (1,)))
            logits = scale * inner + bias
            matched = own_ids == ids_of(number - REACH)
            tail, sigmoid = softplus_parts(logits)
            gradient = sigmoid - matched.astype(F32)
            weights.append((scale * gradient).astype(BF16))
            if with_totals:
                signed = jnp.where(matched, logits, -logits)
                loss = tail - jnp.minimum(signed, 0.0)
                for place, term in enumerate((loss, gradient, gradient * inner)):
                    totals[place] = totals[place] + jnp.sum(term, axis=0, keepdims=True)
        return jnp.concatenate(weights, axis=1), totals

    weight, totals = window_terms(embs[REACH], poses, True)
    grad_img = dot(weight, poses[...].reshape(WINDOW * ROWS, WIDTH), ((1,), (0,)))
    unit_img = unit[...]
    along = jnp.sum(unit_img * grad_img, axis=1, keepdims=True)
    grad_proj = ((grad_img - unit_img * along) * inv_i).astype(BF16)
    for number in range(GROUP):
        gp_src[number] = grad_proj[:, number * COLS : (number + 1) * COLS]
    gp_copies = []
    for step in FAR_FIRST:
        to = mate_slot(step)
        copy = remote(gp_src.at[to], gp.at[slot], gp_s.at[step], gp_r.at[step], base + to)
        copy.start()
        gp_copies.append(copy)
    gp[slot] = gp_src[slot]

    tot_src[...] = jnp.zeros_like(tot_src)
    for place in range(3):
        tot_src[place : place + 1, :] = totals[place]
    tot_copies = []
    for step in FAR_FIRST:
        copy = remote(tot_src, tot_group.at[slot], tot_s.at[step], tot_r.at[step], base + mate_slot(step))
        copy.start()
        tot_copies.append(copy)
    tot_group[slot] = tot_src[...]

    for copy in gp_copies:
        copy.wait_recv()
    emb_direct()
    for of_y in range(SIDE):
        value = dot(feats_t[of_y * ROWS : (of_y + 1) * ROWS, :], gp[...].reshape(GROUP * ROWS, COLS), ((1,), (0,)))
        part_src[of_y * SIDE : (of_y + 1) * SIDE] = value.astype(BF16).reshape(SIDE, TILE, COLS)
    for down, over in PLANE:
        to = lines[down] + spots[over]
        remote(part_src.at[to], part.at[cell], part_s, part_r, to * GROUP + slot).start()
    part[cell] = part_src[cell]
    emb_relay()

    for copy in tot_copies:
        copy.wait_recv()
    group_sum = tot_group[0]
    for number in range(1, GROUP):
        group_sum = group_sum + tot_group[number]
    tot_z_src[...] = group_sum
    tot_z[z] = group_sum
    z_copies = []
    for step in SIDE_FAR_FIRST:
        copy = remote(tot_z_src, tot_z.at[z], tot_s.at[8 + step], tot_r.at[8 + step], at(y, turned(z, step)))
        copy.start()
        z_copies.append(copy)

    emb_forward()
    for copy in z_copies:
        copy.wait_recv()
    z_sum = tot_z[0]
    for number in range(1, SIDE):
        z_sum = z_sum + tot_z[number]
    tot_y_src[...] = z_sum
    tot_y[y] = z_sum
    y_copies = []
    for step in SIDE_FAR_FIRST:
        copy = remote(tot_y_src, tot_y.at[y], tot_s.at[16 + step], tot_r.at[16 + step], at(turned(y, step), z))
        copy.start()
        y_copies.append(copy)

    pltpu.make_async_copy(part.at[pl.ds(0, CELLS - 1)], part.at[pl.ds(0, CELLS - 1)], part_r).wait()

    summed = jnp.sum(part[...].astype(F32), axis=0)
    fin_src[...] = jnp.zeros_like(fin_src)
    for number in range(GROUP):
        fin_src[number, 0:2, :] = summed[2 * number : 2 * number + 2, :]
    fin_copies = []
    for step in FAR_FIRST:
        to = mate_slot(step)
        copy = remote(fin_src.at[to], fin.at[slot], fin_s.at[step], fin_r.at[step], base + to)
        copy.start()
        fin_copies.append(copy)
    fin[slot] = fin_src[slot]

    emb_finish()
    pose_weight, _ = window_terms(poses[REACH], embs, False)
    grad_pose = dot(pose_weight, embs[...].reshape(WINDOW * ROWS, WIDTH), ((1,), (0,)))
    inv_q = inv_pose[:, 0:1]
    unit_pose = pose_raw[...].astype(F32) * inv_q
    along_pose = jnp.sum(unit_pose * grad_pose, axis=1, keepdims=True)
    pose_out[...] = ((grad_pose - unit_pose * along_pose) * inv_q).astype(BF16)
    store_pose = pltpu.make_async_copy(pose_out, pose_grad_hbm, local_sem.at[4])
    store_pose.start()

    for copy in y_copies:
        copy.wait_recv()
    y_sum = tot_y[0]
    for number in range(1, SIDE):
        y_sum = y_sum + tot_y[number]
    y_sum = y_sum / BATCH
    loss_ref[0] = jnp.sum(y_sum[0:1, :])
    loss_ref[1] = jnp.sum(y_sum[1:2, :])
    scale_grad_ref[0] = jnp.sum(y_sum[2:3, :])

    for copy in fin_copies:
        copy.wait_recv()
    for number in range(GROUP):
        head_grad_ref[:, number * COLS : (number + 1) * COLS] = fin[number, 0:2, :]

    store_pose.wait()
    for copy in piece_copies + proj_copies + gp_copies + fin_copies:
        copy.wait_send()
    for copy in tot_copies + z_copies + y_copies:
        copy.wait_send()
    for copy in (right_a, left_b, right_b, left_a, right_a2, left_b2, block_own, block_left, block_right, block_far):
        copy.wait_send()
    pose_drain()
    emb_drain()
    pltpu.make_async_copy(head.at[pl.ds(0, CELLS - 1)], head.at[pl.ds(0, CELLS - 1)], head_s).wait()
    pltpu.make_async_copy(part_src.at[pl.ds(0, CELLS - 1)], part_src.at[pl.ds(0, CELLS - 1)], part_s).wait()


def local(features, head_rows, poses, match_ids, logit_scale, logit_bias):
    vmem = pl.BlockSpec(memory_space=pltpu.VMEM)
    smem = pl.BlockSpec(memory_space=pltpu.SMEM)
    hbm = pl.BlockSpec(memory_space=pltpu.HBM)
    dma = pltpu.SemaphoreType.DMA
    block = (ROWS, WIDTH)
    square = (GROUP, ROWS, COLS)
    shapes = (
        jax.ShapeDtypeStruct(block, BF16),
        jax.ShapeDtypeStruct((2, WIDTH), F32),
        jax.ShapeDtypeStruct((2,), F32),
        jax.ShapeDtypeStruct((1,), F32),
    )
    return pl.pallas_call(
        kernel,
        name="contrastive",
        out_shape=shapes,
        in_specs=[hbm, hbm, hbm, hbm, vmem, vmem],
        out_specs=(hbm, vmem, smem, smem),
        scratch_shapes=[
            pltpu.VMEM((GROUP,) + block, BF16),
            pltpu.VMEM((WIDTH, GROUP * ROWS), BF16),
            pltpu.VMEM(block, BF16),
            pltpu.VMEM((WINDOW,) + block, BF16),
            pltpu.VMEM((WINDOW,) + block, BF16),
            pltpu.VMEM(block, BF16),
            pltpu.VMEM(block, BF16),
            pltpu.VMEM(block, BF16),
            pltpu.VMEM((COUNT, ROWS), jnp.int32),
            pltpu.VMEM((2, WIDTH), BF16),
            pltpu.VMEM((GROUP, 8, COLS), F32),
            pltpu.VMEM((GROUP, 8, COLS), F32),
            pltpu.VMEM((TILE, COLS), F32),
            pltpu.VMEM((CELLS, TILE, COLS), BF16),
            pltpu.VMEM(square, F32),
            pltpu.VMEM(square, F32),
            pltpu.VMEM(block, F32),
            pltpu.VMEM((ROWS, COLS), F32),
            pltpu.VMEM(square, BF16),
            pltpu.VMEM(square, BF16),
            pltpu.VMEM((CELLS, TILE, COLS), BF16),
            pltpu.VMEM((CELLS, TILE, COLS), BF16),
            pltpu.VMEM((GROUP, 8, COLS), F32),
            pltpu.VMEM((GROUP, 8, COLS), F32),
            pltpu.VMEM((8, COLS), F32),
            pltpu.VMEM((GROUP, 8, COLS), F32),
            pltpu.VMEM((8, COLS), F32),
            pltpu.VMEM((SIDE, 8, COLS), F32),
            pltpu.VMEM((8, COLS), F32),
            pltpu.VMEM((SIDE, 8, COLS), F32),
            dma((5,)),
            dma((GROUP,)), dma((GROUP,)),
            dma((10,)), dma((10,)),
            dma, dma,
            dma((WINDOW,)), dma((WINDOW,)),
            dma((WINDOW,)), dma((WINDOW,)),
            dma((GROUP,)), dma((GROUP,)),
            dma((GROUP,)), dma((GROUP,)),
            dma, dma,
            dma((GROUP,)), dma((GROUP,)),
            dma((24,)), dma((24,)),
        ],
        compiler_params=pltpu.CompilerParams(
            collective_id=0, has_side_effects=True, vmem_limit_bytes=53 * 1024 * 1024 + 512 * 1024
        ),
    )(features, head_rows, poses, match_ids.reshape(COUNT, ROWS), logit_scale.reshape(1, 1), logit_bias.reshape(1, 1))


def solution(mesh):
    return jax.shard_map(
        local,
        mesh=mesh,
        in_specs=(P("dp", None), P("dp", None), P("dp", None), P(), P(), P()),
        out_specs=(P("dp", None), P("dp", None), P(), P()),
        check_vma=False,
    )
```

```python
import jax
import jax.numpy as jnp
from jax import lax
from jax.experimental import pallas as pl
from jax.experimental.pallas import tpu as pltpu
from jax.sharding import PartitionSpec as P

REACH = 2
WINDOW = 2 * REACH + 1
EPS = 1e-06
ROWS = 128
COLS = 128
GROUP = 8
SIDE = 8
CELLS = SIDE * SIDE
COUNT = GROUP * CELLS
BATCH = ROWS * COUNT
WIDTH = GROUP * COLS
TILE = 16
HALF = ROWS // 2
LEVELS = 32767.0
SMALLEST = 1e-33
FAR_FIRST = (4, 5, 3, 2, 6, 7, 1)
SIDE_FAR_FIRST = (4, 3, 5, 2, 6, 1, 7)
PLANE = [(down, over) for down in SIDE_FAR_FIRST + (0,) for over in SIDE_FAR_FIRST + (0,) if down or over]

F32 = jnp.float32
BF16 = jnp.bfloat16


def remote(src, dst, send_sem, recv_sem, device):
    return pltpu.make_async_remote_copy(
        src_ref=src,
        dst_ref=dst,
        send_sem=send_sem,
        recv_sem=recv_sem,
        device_id=(device,),
        device_id_type=pl.DeviceIdType.MESH,
    )


def dot(left, right, dims):
    return lax.dot_general(left, right, (dims, ((), ())), preferred_element_type=F32)


def softplus_parts(logits):
    tail = jnp.exp(-jnp.abs(logits))
    share = 1.0 / (1.0 + tail)
    sigmoid = jnp.where(logits >= 0, share, tail * share)
    return jnp.log1p(tail), sigmoid


def kernel(
    feat_hbm, head_hbm, pose_hbm, ids_hbm, scale_ref, bias_ref,
    pose_grad_hbm, head_grad_ref, loss_ref, scale_grad_ref,
    feats, feats_t, pose_raw, poses, embs, pose_held, emb_held, pose_out, ids, head_rows, piece_src, piece, tile_f32, head,
    proj_src, proj, peak_src, peaks, peak_rows, unit, inv_pose, gp_src, gp, part_src, part, fin_src, fin,
    tot_src, tot_group, tot_z_src, tot_z, tot_y_src, tot_y,
    local_sem, piece_s, piece_r, feat_s, feat_r, head_s, head_r, pose_s, pose_r, emb_s, emb_r,
    proj_s, proj_r, gp_s, gp_r, part_s, part_r, fin_s, fin_r, tot_s, tot_r,
):
    me = lax.axis_index("dp")
    slot = lax.rem(me, GROUP)
    cell = me // GROUP
    y = cell // SIDE
    z = lax.rem(cell, SIDE)
    core = lax.rem(me, 2)
    base = me - slot
    sibling = me + 1 - 2 * core
    lines = [lax.rem(y + step, SIDE) * SIDE for step in range(SIDE)]
    spots = [lax.rem(z + step, SIDE) for step in range(SIDE)]

    def mate_slot(step):
        return lax.rem(slot + step, GROUP)

    def turned(place, step):
        return lax.rem(place + step, SIDE)

    def at(of_y, of_z):
        return (of_y * SIDE + of_z) * GROUP + slot

    def ring(step):
        return lax.rem(me + step + COUNT, COUNT)

    loads = [
        pltpu.make_async_copy(source, target, local_sem.at[number])
        for number, (source, target) in enumerate((
            (head_hbm, head_rows),
            (feat_hbm, feats.at[slot]),
            (pose_hbm, pose_raw),
            (ids_hbm, ids),
        ))
    ]
    load_head, load_feat, load_pose, load_ids = loads
    for load in loads:
        load.start()

    barrier = pltpu.get_barrier_semaphore()

    def greet(device):
        pl.semaphore_signal(barrier, inc=1, device_id=(device,), device_id_type=pl.DeviceIdType.MESH)

    for step in FAR_FIRST:
        greet(base + mate_slot(step))
    for down, over in PLANE:
        greet((lines[down] + spots[over]) * GROUP + slot)

    peak_rows[...] = jnp.zeros_like(peak_rows)
    load_head.wait()
    rows = head_rows[...].astype(F32)
    piece_src[...] = jnp.zeros_like(piece_src)
    for number in range(GROUP):
        piece_src[number, 0:2, :] = rows[:, number * COLS : (number + 1) * COLS]
    piece[slot] = piece_src[slot]

    pl.semaphore_wait(barrier, GROUP - 1 + CELLS - 1)

    def exchange(blocks, held, sems, semr):
        def part_of(place, number):
            return blocks.at[place, pl.ds(number * HALF, HALF), :]

        def pair(make):
            return [make(number) for number in range(2)]

        def held_part(number):
            return held.at[pl.ds(number * HALF, HALF), :]

        last = GROUP - 2
        ahead = pair(lambda n: remote(part_of(REACH, n), part_of(0, n), sems.at[n], semr.at[n], ring(2)))
        behind = pair(lambda n: remote(part_of(REACH, n), part_of(4, n), sems.at[2 + n], semr.at[8 + n], ring(-2)))
        ahead_cell = pair(lambda n: remote(part_of(REACH, n), held_part(n), sems.at[n], semr.at[4 + n], ring(GROUP)))
        behind_cell = pair(
            lambda n: remote(part_of(REACH, n), held_part(n), sems.at[2 + n], semr.at[4 + n], ring(-GROUP))
        )
        ahead_relay = pair(lambda n: remote(held_part(n), part_of(0, n), sems.at[8 + n], semr.at[n], base + core))
        behind_relay = pair(
            lambda n: remote(held_part(n), part_of(4, n), sems.at[8 + n], semr.at[8 + n], base + last + core)
        )
        to_own = 1 + 2 * core
        to_pass = 3 - 2 * core
        beside = pair(
            lambda n: remote(part_of(REACH, n), part_of(to_own, n), sems.at[4 + n], semr.at[2 * to_own + n], sibling)
        )
        far = 4 - 4 * core
        passed = pair(
            lambda n: remote(part_of(far, n), part_of(to_pass, n), sems.at[6 + n], semr.at[2 * to_pass + n], sibling)
        )

        def arrived(place, number):
            remote(part_of(REACH, number), part_of(place, number), sems.at[0], semr.at[2 * place + number], sibling).wait_recv()

        def to_cells():
            for number in range(2):
                pl.when(slot >= last)(ahead_cell[number].start)
                pl.when(slot < 2)(behind_cell[number].start)

        def direct():
            for number in range(2):
                pl.when(slot < last)(ahead[number].start)
                pl.when(slot >= 2)(behind[number].start)
            for number in range(2):
                beside[number].start()

        def relay(number):
            @pl.when(slot >= last)
            def _():
                ahead_cell[number].wait_recv()
                ahead_relay[number].start()

            @pl.when(slot < 2)
            def _():
                behind_cell[number].wait_recv()
                behind_relay[number].start()

        def forward(number):
            arrived(far, number)
            passed[number].start()

        def finish():
            for number in range(2):
                for place in (4 * core, 1, 3):
                    arrived(place, number)

        def drain():
            for number in range(2):
                for copies in (ahead, behind, beside, passed):
                    copies[number].wait_send()
                pl.when(slot >= last)(ahead_relay[number].wait_send)
                pl.when(slot < 2)(behind_relay[number].wait_send)

        return to_cells, direct, relay, forward, finish, drain

    pose_to_cells, pose_direct, pose_relay, pose_forward, pose_finish, pose_drain = exchange(
        poses, pose_held, pose_s, pose_r
    )
    emb_to_cells, emb_direct, emb_relay, emb_forward, emb_finish, emb_drain = exchange(embs, emb_held, emb_s, emb_r)

    piece_copies = []
    for step in FAR_FIRST:
        to = mate_slot(step)
        copy = remote(piece_src.at[to], piece.at[slot], piece_s.at[step], piece_r.at[step], base + to)
        copy.start()
        piece_copies.append(copy)

    load_feat.wait()
    right = base + mate_slot(2)
    left = base + mate_slot(6)

    def half(of_slot, number):
        return feats.at[of_slot, pl.ds(number * HALF, HALF), :]

    def send_half(of_slot, number, device, sem):
        copy = remote(half(of_slot, number), half(of_slot, number), feat_s.at[sem], feat_r.at[sem], device)
        copy.start()
        return copy

    def send_block(of_slot, sem):
        copy = remote(feats.at[of_slot], feats.at[of_slot], feat_s.at[sem], feat_r.at[sem], sibling)
        copy.start()
        return copy

    right_a = send_half(slot, 0, right, 0)
    left_b = send_half(slot, 1, left, 1)
    right_b = send_half(slot, 1, right, 2)
    left_a = send_half(slot, 0, left, 3)
    block_own = send_block(slot, 6)

    load_pose.wait()
    raw = pose_raw[...].astype(F32)
    inv_p = 1.0 / jnp.sqrt(jnp.sum(raw * raw, axis=1, keepdims=True) + EPS)
    inv_pose[...] = jnp.broadcast_to(inv_p, (ROWS, COLS))
    poses[REACH] = (raw * inv_p).astype(BF16)
    pose_to_cells()

    for copy in piece_copies:
        copy.wait_recv()
    for number in range(GROUP):
        tile_f32[2 * number : 2 * number + 2, :] = piece[number, 0:2, :]
    head[cell] = tile_f32[...].astype(BF16)
    for down, over in PLANE:
        device = (lines[down] + spots[over]) * GROUP + slot
        remote(head.at[cell], head.at[cell], head_s, head_r, device).start()

    right_a.wait_recv()
    right_a2 = send_half(mate_slot(6), 0, right, 4)
    left_b.wait_recv()
    left_b2 = send_half(mate_slot(2), 1, left, 5)

    pose_direct()
    pose_relay(0)
    pose_relay(1)

    right_b.wait_recv()
    block_left = send_block(mate_slot(6), 7)
    left_a.wait_recv()
    block_right = send_block(mate_slot(2), 8)
    right_a2.wait_recv()
    left_b2.wait_recv()
    block_far = send_block(mate_slot(4), 9)

    pltpu.make_async_copy(head.at[pl.ds(0, CELLS - 1)], head.at[pl.ds(0, CELLS - 1)], head_r).wait()
    for copy in (block_own, block_left, block_right, block_far):
        copy.wait_recv()
    lane = lax.broadcasted_iota(jnp.int32, (ROWS, COLS), 1)
    peak_columns = jnp.zeros((ROWS, COLS), F32)
    proj_copies = []
    for step in FAR_FIRST + (0,):
        to = mate_slot(step)
        value = dot(feats[to], head[...].reshape(WIDTH, COLS), ((1,), (0,)))
        peak = jnp.maximum(jnp.max(jnp.abs(value), axis=1, keepdims=True), SMALLEST)
        coded = jnp.round(value * (LEVELS / peak)).astype(jnp.int32).astype(jnp.int16)
        peak_columns = jnp.where(lane == to, peak, peak_columns)
        if step:
            proj_src[step] = coded
            copy = remote(proj_src.at[step], proj.at[slot], proj_s.at[step], proj_r.at[step], base + to)
            copy.start()
            proj_copies.append(copy)
        else:
            proj[slot] = coded
    peak_src[...] = peak_columns.T[0:GROUP, :]
    peaks[slot] = peak_src[...]
    for step in FAR_FIRST:
        copy = remote(
            peak_src, peaks.at[slot], proj_s.at[GROUP + step], proj_r.at[GROUP + step], base + mate_slot(step)
        )
        copy.start()
        proj_copies.append(copy)

    pose_forward(0)
    pose_forward(1)
    for number in range(GROUP):
        feats_t[:, number * ROWS : (number + 1) * ROWS] = feats[number].T
    load_ids.wait()
    pose_finish()
    for copy in proj_copies:
        copy.wait_recv()

    for number in range(GROUP):
        peak_rows[number : number + 1, :] = peaks[number, pl.ds(slot, 1), :]
    unscale = peak_rows[...].T / LEVELS
    square = jnp.zeros((ROWS, COLS), F32)
    for number in range(GROUP):
        value = proj[number].astype(jnp.int32).astype(F32) * unscale[:, number : number + 1]
        unit[:, number * COLS : (number + 1) * COLS] = value
        square = square + value * value
    inv_i = 1.0 / jnp.sqrt(jnp.sum(square, axis=1, keepdims=True) + EPS)
    for number in range(GROUP):
        columns = slice(number * COLS, (number + 1) * COLS)
        value = unit[:, columns] * inv_i
        unit[:, columns] = value
        embs[REACH, :, columns] = value.astype(BF16)
    emb_to_cells()

    scale = jnp.broadcast_to(scale_ref[...], (ROWS, ROWS))
    bias = jnp.broadcast_to(bias_ref[...], (ROWS, ROWS))

    def ids_of(step):
        return ids[pl.ds(ring(step), 1), :]

    own_ids = jnp.broadcast_to(ids_of(0), (ROWS, ROWS)).T

    def window_terms(left_emb, blocks, with_totals):
        weights = []
        totals = [jnp.zeros((1, COLS), F32) for _ in range(3)]
        for number in range(WINDOW):
            inner = dot(left_emb, blocks[number], ((1,), (1,)))
            logits = scale * inner + bias
            matched = own_ids == ids_of(number - REACH)
            tail, sigmoid = softplus_parts(logits)
            gradient = sigmoid - matched.astype(F32)
            weights.append((scale * gradient).astype(BF16))
            if with_totals:
                signed = jnp.where(matched, logits, -logits)
                loss = tail - jnp.minimum(signed, 0.0)
                for place, term in enumerate((loss, gradient, gradient * inner)):
                    totals[place] = totals[place] + jnp.sum(term, axis=0, keepdims=True)
        return jnp.concatenate(weights, axis=1), totals

    weight, totals = window_terms(embs[REACH], poses, True)
    grad_img = dot(weight, poses[...].reshape(WINDOW * ROWS, WIDTH), ((1,), (0,)))
    unit_img = unit[...]
    along = jnp.sum(unit_img * grad_img, axis=1, keepdims=True)
    grad_proj = ((grad_img - unit_img * along) * inv_i).astype(BF16)
    for number in range(GROUP):
        gp_src[number] = grad_proj[:, number * COLS : (number + 1) * COLS]
    gp_copies = []
    for step in FAR_FIRST:
        to = mate_slot(step)
        copy = remote(gp_src.at[to], gp.at[slot], gp_s.at[step], gp_r.at[step], base + to)
        copy.start()
        gp_copies.append(copy)
    gp[slot] = gp_src[slot]

    tot_src[...] = jnp.zeros_like(tot_src)
    for place in range(3):
        tot_src[place : place + 1, :] = totals[place]
    tot_copies = []
    for step in FAR_FIRST:
        copy = remote(tot_src, tot_group.at[slot], tot_s.at[step], tot_r.at[step], base + mate_slot(step))
        copy.start()
        tot_copies.append(copy)
    tot_group[slot] = tot_src[...]

    for copy in gp_copies:
        copy.wait_recv()
    emb_direct()
    emb_relay(0)
    for of_y in range(SIDE):
        value = dot(feats_t[of_y * ROWS : (of_y + 1) * ROWS, :], gp[...].reshape(GROUP * ROWS, COLS), ((1,), (0,)))
        part_src[of_y * SIDE : (of_y + 1) * SIDE] = value.astype(BF16).reshape(SIDE, TILE, COLS)
    for down, over in PLANE:
        to = lines[down] + spots[over]
        remote(part_src.at[to], part.at[cell], part_s, part_r, to * GROUP + slot).start()
    part[cell] = part_src[cell]
    emb_relay(1)

    for copy in tot_copies:
        copy.wait_recv()
    group_sum = tot_group[0]
    for number in range(1, GROUP):
        group_sum = group_sum + tot_group[number]
    tot_z_src[...] = group_sum
    tot_z[z] = group_sum
    z_copies = []
    for step in SIDE_FAR_FIRST:
        copy = remote(tot_z_src, tot_z.at[z], tot_s.at[8 + step], tot_r.at[8 + step], at(y, turned(z, step)))
        copy.start()
        z_copies.append(copy)

    emb_forward(0)
    emb_forward(1)
    for copy in z_copies:
        copy.wait_recv()
    z_sum = tot_z[0]
    for number in range(1, SIDE):
        z_sum = z_sum + tot_z[number]
    tot_y_src[...] = z_sum
    tot_y[y] = z_sum
    y_copies = []
    for step in SIDE_FAR_FIRST:
        copy = remote(tot_y_src, tot_y.at[y], tot_s.at[16 + step], tot_r.at[16 + step], at(turned(y, step), z))
        copy.start()
        y_copies.append(copy)

    pltpu.make_async_copy(part.at[pl.ds(0, CELLS - 1)], part.at[pl.ds(0, CELLS - 1)], part_r).wait()

    summed = jnp.sum(part[...].astype(F32), axis=0)
    fin_src[...] = jnp.zeros_like(fin_src)
    for number in range(GROUP):
        fin_src[number, 0:2, :] = summed[2 * number : 2 * number + 2, :]
    fin_copies = []
    for step in FAR_FIRST:
        to = mate_slot(step)
        copy = remote(fin_src.at[to], fin.at[slot], fin_s.at[step], fin_r.at[step], base + to)
        copy.start()
        fin_copies.append(copy)
    fin[slot] = fin_src[slot]

    emb_finish()
    pose_weight, _ = window_terms(poses[REACH], embs, False)
    grad_pose = dot(pose_weight, embs[...].reshape(WINDOW * ROWS, WIDTH), ((1,), (0,)))
    inv_q = inv_pose[:, 0:1]
    unit_pose = pose_raw[...].astype(F32) * inv_q
    along_pose = jnp.sum(unit_pose * grad_pose, axis=1, keepdims=True)
    pose_out[...] = ((grad_pose - unit_pose * along_pose) * inv_q).astype(BF16)
    store_pose = pltpu.make_async_copy(pose_out, pose_grad_hbm, local_sem.at[4])
    store_pose.start()

    for copy in y_copies:
        copy.wait_recv()
    y_sum = tot_y[0]
    for number in range(1, SIDE):
        y_sum = y_sum + tot_y[number]
    y_sum = y_sum / BATCH
    loss_ref[0] = jnp.sum(y_sum[0:1, :])
    loss_ref[1] = jnp.sum(y_sum[1:2, :])
    scale_grad_ref[0] = jnp.sum(y_sum[2:3, :])

    for copy in fin_copies:
        copy.wait_recv()
    for number in range(GROUP):
        head_grad_ref[:, number * COLS : (number + 1) * COLS] = fin[number, 0:2, :]

    store_pose.wait()
    for copy in piece_copies + proj_copies + gp_copies + fin_copies:
        copy.wait_send()
    for copy in tot_copies + z_copies + y_copies:
        copy.wait_send()
    for copy in (right_a, left_b, right_b, left_a, right_a2, left_b2, block_own, block_left, block_right, block_far):
        copy.wait_send()
    pose_drain()
    emb_drain()
    pltpu.make_async_copy(head.at[pl.ds(0, CELLS - 1)], head.at[pl.ds(0, CELLS - 1)], head_s).wait()
    pltpu.make_async_copy(part_src.at[pl.ds(0, CELLS - 1)], part_src.at[pl.ds(0, CELLS - 1)], part_s).wait()


def local(features, head_rows, poses, match_ids, logit_scale, logit_bias):
    vmem = pl.BlockSpec(memory_space=pltpu.VMEM)
    smem = pl.BlockSpec(memory_space=pltpu.SMEM)
    hbm = pl.BlockSpec(memory_space=pltpu.HBM)
    dma = pltpu.SemaphoreType.DMA
    block = (ROWS, WIDTH)
    square = (GROUP, ROWS, COLS)
    shapes = (
        jax.ShapeDtypeStruct(block, BF16),
        jax.ShapeDtypeStruct((2, WIDTH), F32),
        jax.ShapeDtypeStruct((2,), F32),
        jax.ShapeDtypeStruct((1,), F32),
    )
    return pl.pallas_call(
        kernel,
        name="contrastive",
        out_shape=shapes,
        in_specs=[hbm, hbm, hbm, hbm, vmem, vmem],
        out_specs=(hbm, vmem, smem, smem),
        scratch_shapes=[
            pltpu.VMEM((GROUP,) + block, BF16),
            pltpu.VMEM((WIDTH, GROUP * ROWS), BF16),
            pltpu.VMEM(block, BF16),
            pltpu.VMEM((WINDOW,) + block, BF16),
            pltpu.VMEM((WINDOW,) + block, BF16),
            pltpu.VMEM(block, BF16),
            pltpu.VMEM(block, BF16),
            pltpu.VMEM(block, BF16),
            pltpu.VMEM((COUNT, ROWS), jnp.int32),
            pltpu.VMEM((2, WIDTH), BF16),
            pltpu.VMEM((GROUP, 8, COLS), F32),
            pltpu.VMEM((GROUP, 8, COLS), F32),
            pltpu.VMEM((TILE, COLS), F32),
            pltpu.VMEM((CELLS, TILE, COLS), BF16),
            pltpu.VMEM(square, jnp.int16),
            pltpu.VMEM(square, jnp.int16),
            pltpu.VMEM((GROUP, COLS), F32),
            pltpu.VMEM((GROUP, GROUP, COLS), F32),
            pltpu.VMEM((ROWS, COLS), F32),
            pltpu.VMEM(block, F32),
            pltpu.VMEM((ROWS, COLS), F32),
            pltpu.VMEM(square, BF16),
            pltpu.VMEM(square, BF16),
            pltpu.VMEM((CELLS, TILE, COLS), BF16),
            pltpu.VMEM((CELLS, TILE, COLS), BF16),
            pltpu.VMEM((GROUP, 8, COLS), F32),
            pltpu.VMEM((GROUP, 8, COLS), F32),
            pltpu.VMEM((8, COLS), F32),
            pltpu.VMEM((GROUP, 8, COLS), F32),
            pltpu.VMEM((8, COLS), F32),
            pltpu.VMEM((SIDE, 8, COLS), F32),
            pltpu.VMEM((8, COLS), F32),
            pltpu.VMEM((SIDE, 8, COLS), F32),
            dma((5,)),
            dma((GROUP,)), dma((GROUP,)),
            dma((10,)), dma((10,)),
            dma, dma,
            dma((2 * WINDOW,)), dma((2 * WINDOW,)),
            dma((2 * WINDOW,)), dma((2 * WINDOW,)),
            dma((2 * GROUP,)), dma((2 * GROUP,)),
            dma((GROUP,)), dma((GROUP,)),
            dma, dma,
            dma((GROUP,)), dma((GROUP,)),
            dma((24,)), dma((24,)),
        ],
        compiler_params=pltpu.CompilerParams(
            collective_id=0, has_side_effects=True, vmem_limit_bytes=53 * 1024 * 1024 + 512 * 1024
        ),
    )(features, head_rows, poses, match_ids.reshape(COUNT, ROWS), logit_scale.reshape(1, 1), logit_bias.reshape(1, 1))


def solution(mesh):
    return jax.shard_map(
        local,
        mesh=mesh,
        in_specs=(P("dp", None), P("dp", None), P("dp", None), P(), P(), P()),
        out_specs=(P("dp", None), P("dp", None), P(), P()),
        check_vma=False,
    )
```

```python
import jax
import jax.numpy as jnp
from jax import lax
from jax.experimental import pallas as pl
from jax.experimental.pallas import tpu as pltpu
from jax.sharding import PartitionSpec as P

REACH = 2
WINDOW = 2 * REACH + 1
EPS = 1e-06
ROWS = 128
COLS = 128
GROUP = 8
SIDE = 8
CELLS = SIDE * SIDE
COUNT = GROUP * CELLS
BATCH = ROWS * COUNT
WIDTH = GROUP * COLS
TILE = 16
HALF = ROWS // 2
LEVELS = 32767.0
SMALLEST = 1e-33
FAR_FIRST = (4, 5, 3, 2, 6, 7, 1)
SIDE_FAR_FIRST = (4, 3, 5, 2, 6, 1, 7)
PLANE = [(down, over) for down in SIDE_FAR_FIRST + (0,) for over in SIDE_FAR_FIRST + (0,) if down or over]

F32 = jnp.float32
BF16 = jnp.bfloat16


def remote(src, dst, send_sem, recv_sem, device):
    return pltpu.make_async_remote_copy(
        src_ref=src,
        dst_ref=dst,
        send_sem=send_sem,
        recv_sem=recv_sem,
        device_id=(device,),
        device_id_type=pl.DeviceIdType.MESH,
    )


def dot(left, right, dims):
    return lax.dot_general(left, right, (dims, ((), ())), preferred_element_type=F32)


def softplus_parts(logits):
    tail = jnp.exp(-jnp.abs(logits))
    share = 1.0 / (1.0 + tail)
    sigmoid = jnp.where(logits >= 0, share, tail * share)
    return jnp.log1p(tail), sigmoid


def kernel(
    feat_hbm, head_hbm, pose_hbm, ids_hbm, scale_ref, bias_ref,
    pose_grad_hbm, head_grad_ref, loss_ref, scale_grad_ref,
    feats, feats_t, pose_raw, poses, embs, pose_held, emb_held, pose_out, ids, head_rows, piece_src, piece, tile_f32, head,
    proj_src, proj, peak_src, peaks, peak_rows, unit, inv_pose, gp_src, gp, part_src, part, fin_src, fin,
    tot_src, tot_group, tot_z_src, tot_z, tot_y_src, tot_y,
    local_sem, piece_s, piece_r, feat_s, feat_r, head_s, head_r, pose_s, pose_r, emb_s, emb_r,
    proj_s, proj_r, gp_s, gp_r, part_s, part_r, fin_s, fin_r, tot_s, tot_r,
):
    me = lax.axis_index("dp")
    slot = lax.rem(me, GROUP)
    cell = me // GROUP
    y = cell // SIDE
    z = lax.rem(cell, SIDE)
    core = lax.rem(me, 2)
    base = me - slot
    sibling = me + 1 - 2 * core
    lines = [lax.rem(y + step, SIDE) * SIDE for step in range(SIDE)]
    spots = [lax.rem(z + step, SIDE) for step in range(SIDE)]

    def mate_slot(step):
        return lax.rem(slot + step, GROUP)

    def turned(place, step):
        return lax.rem(place + step, SIDE)

    def at(of_y, of_z):
        return (of_y * SIDE + of_z) * GROUP + slot

    def ring(step):
        return lax.rem(me + step + COUNT, COUNT)

    loads = [
        pltpu.make_async_copy(source, target, local_sem.at[number])
        for number, (source, target) in enumerate((
            (head_hbm, head_rows),
            (feat_hbm, feats.at[slot]),
            (pose_hbm, pose_raw),
            (ids_hbm, ids),
        ))
    ]
    load_head, load_feat, load_pose, load_ids = loads
    for load in loads:
        load.start()

    barrier = pltpu.get_barrier_semaphore()

    def greet(device):
        pl.semaphore_signal(barrier, inc=1, device_id=(device,), device_id_type=pl.DeviceIdType.MESH)

    for step in FAR_FIRST:
        greet(base + mate_slot(step))
    for down, over in PLANE:
        greet((lines[down] + spots[over]) * GROUP + slot)

    peak_rows[...] = jnp.zeros_like(peak_rows)
    load_head.wait()
    rows = head_rows[...].astype(F32)
    piece_src[...] = jnp.zeros_like(piece_src)
    for number in range(GROUP):
        piece_src[number, 0:2, :] = rows[:, number * COLS : (number + 1) * COLS]
    piece[slot] = piece_src[slot]

    pl.semaphore_wait(barrier, GROUP - 1 + CELLS - 1)

    def exchange(blocks, held, sems, semr):
        def part_of(place, number):
            return blocks.at[place, pl.ds(number * HALF, HALF), :]

        def pair(make):
            return [make(number) for number in range(2)]

        def held_part(number):
            return held.at[pl.ds(number * HALF, HALF), :]

        last = GROUP - 2
        ahead = pair(lambda n: remote(part_of(REACH, n), part_of(0, n), sems.at[n], semr.at[n], ring(2)))
        behind = pair(lambda n: remote(part_of(REACH, n), part_of(4, n), sems.at[2 + n], semr.at[8 + n], ring(-2)))
        ahead_cell = pair(lambda n: remote(part_of(REACH, n), held_part(n), sems.at[n], semr.at[4 + n], ring(GROUP)))
        behind_cell = pair(
            lambda n: remote(part_of(REACH, n), held_part(n), sems.at[2 + n], semr.at[4 + n], ring(-GROUP))
        )
        ahead_relay = pair(lambda n: remote(held_part(n), part_of(0, n), sems.at[8 + n], semr.at[n], base + core))
        behind_relay = pair(
            lambda n: remote(held_part(n), part_of(4, n), sems.at[8 + n], semr.at[8 + n], base + last + core)
        )
        to_own = 1 + 2 * core
        to_pass = 3 - 2 * core
        beside = pair(
            lambda n: remote(part_of(REACH, n), part_of(to_own, n), sems.at[4 + n], semr.at[2 * to_own + n], sibling)
        )
        far = 4 - 4 * core
        passed = pair(
            lambda n: remote(part_of(far, n), part_of(to_pass, n), sems.at[6 + n], semr.at[2 * to_pass + n], sibling)
        )

        def arrived(place, number):
            remote(part_of(REACH, number), part_of(place, number), sems.at[0], semr.at[2 * place + number], sibling).wait_recv()

        def to_cells():
            for number in range(2):
                pl.when(slot >= last)(ahead_cell[number].start)
                pl.when(slot < 2)(behind_cell[number].start)

        def direct():
            for number in range(2):
                pl.when(slot < last)(ahead[number].start)
                pl.when(slot >= 2)(behind[number].start)
            for number in range(2):
                beside[number].start()

        def relay(number):
            @pl.when(slot >= last)
            def _():
                ahead_cell[number].wait_recv()
                ahead_relay[number].start()

            @pl.when(slot < 2)
            def _():
                behind_cell[number].wait_recv()
                behind_relay[number].start()

        def forward(number):
            arrived(far, number)
            passed[number].start()

        def finish():
            for number in range(2):
                for place in (4 * core, 1, 3):
                    arrived(place, number)

        def drain():
            for number in range(2):
                for copies in (ahead, behind, beside, passed):
                    copies[number].wait_send()
                pl.when(slot >= last)(ahead_relay[number].wait_send)
                pl.when(slot < 2)(behind_relay[number].wait_send)

        return to_cells, direct, relay, forward, finish, drain

    pose_to_cells, pose_direct, pose_relay, pose_forward, pose_finish, pose_drain = exchange(
        poses, pose_held, pose_s, pose_r
    )
    emb_to_cells, emb_direct, emb_relay, emb_forward, emb_finish, emb_drain = exchange(embs, emb_held, emb_s, emb_r)

    piece_copies = []
    for step in FAR_FIRST:
        to = mate_slot(step)
        copy = remote(piece_src.at[to], piece.at[slot], piece_s.at[step], piece_r.at[step], base + to)
        copy.start()
        piece_copies.append(copy)

    load_feat.wait()
    right = base + mate_slot(2)
    left = base + mate_slot(6)

    def half(of_slot, number):
        return feats.at[of_slot, pl.ds(number * HALF, HALF), :]

    def send_half(of_slot, number, device, sem):
        copy = remote(half(of_slot, number), half(of_slot, number), feat_s.at[sem], feat_r.at[sem], device)
        copy.start()
        return copy

    def send_block(of_slot, sem):
        copy = remote(feats.at[of_slot], feats.at[of_slot], feat_s.at[sem], feat_r.at[sem], sibling)
        copy.start()
        return copy

    right_a = send_half(slot, 0, right, 0)
    left_b = send_half(slot, 1, left, 1)
    right_b = send_half(slot, 1, right, 2)
    left_a = send_half(slot, 0, left, 3)
    block_own = send_block(slot, 6)

    load_pose.wait()
    raw = pose_raw[...].astype(F32)
    inv_p = 1.0 / jnp.sqrt(jnp.sum(raw * raw, axis=1, keepdims=True) + EPS)
    inv_pose[...] = jnp.broadcast_to(inv_p, (ROWS, COLS))
    poses[REACH] = (raw * inv_p).astype(BF16)
    pose_to_cells()

    for copy in piece_copies:
        copy.wait_recv()
    for number in range(GROUP):
        tile_f32[2 * number : 2 * number + 2, :] = piece[number, 0:2, :]
    head[cell] = tile_f32[...].astype(BF16)
    for down, over in PLANE:
        device = (lines[down] + spots[over]) * GROUP + slot
        remote(head.at[cell], head.at[cell], head_s, head_r, device).start()

    right_a.wait_recv()
    right_a2 = send_half(mate_slot(6), 0, right, 4)
    left_b.wait_recv()
    left_b2 = send_half(mate_slot(2), 1, left, 5)

    pose_direct()
    pose_relay(0)
    pose_relay(1)

    right_b.wait_recv()
    block_left = send_block(mate_slot(6), 7)
    left_a.wait_recv()
    block_right = send_block(mate_slot(2), 8)
    right_a2.wait_recv()
    left_b2.wait_recv()
    block_far = send_block(mate_slot(4), 9)

    pltpu.make_async_copy(head.at[pl.ds(0, CELLS - 1)], head.at[pl.ds(0, CELLS - 1)], head_r).wait()
    for copy in (block_own, block_left, block_right, block_far):
        copy.wait_recv()
    lane = lax.broadcasted_iota(jnp.int32, (ROWS, COLS), 1)
    peak_columns = jnp.zeros((ROWS, COLS), F32)
    proj_copies = []
    for step in FAR_FIRST + (0,):
        to = mate_slot(step)
        value = dot(feats[to], head[...].reshape(WIDTH, COLS), ((1,), (0,)))
        peak = jnp.maximum(jnp.max(jnp.abs(value), axis=1, keepdims=True), SMALLEST)
        coded = jnp.round(value * (LEVELS / peak)).astype(jnp.int32).astype(jnp.int16)
        peak_columns = jnp.where(lane == to, peak, peak_columns)
        if step:
            proj_src[step] = coded
            copy = remote(proj_src.at[step], proj.at[slot], proj_s.at[step], proj_r.at[step], base + to)
            copy.start()
            proj_copies.append(copy)
        else:
            proj[slot] = coded
    peak_src[...] = peak_columns.T[0:GROUP, :]
    peaks[slot] = peak_src[...]
    for step in FAR_FIRST:
        copy = remote(
            peak_src, peaks.at[slot], proj_s.at[GROUP + step], proj_r.at[GROUP + step], base + mate_slot(step)
        )
        copy.start()
        proj_copies.append(copy)

    pose_forward(0)
    pose_forward(1)
    for number in range(GROUP):
        feats_t[:, number * ROWS : (number + 1) * ROWS] = feats[number].T
    load_ids.wait()
    scale = jnp.broadcast_to(scale_ref[...], (ROWS, ROWS))
    bias = jnp.broadcast_to(bias_ref[...], (ROWS, ROWS))

    def ids_of(step):
        return ids[pl.ds(ring(step), 1), :]

    own_ids = jnp.broadcast_to(ids_of(0), (ROWS, ROWS)).T
    tot_src[...] = jnp.zeros_like(tot_src)
    fin_src[...] = jnp.zeros_like(fin_src)
    pose_finish()
    for copy in proj_copies:
        copy.wait_recv()

    for number in range(GROUP):
        peak_rows[number : number + 1, :] = peaks[number, pl.ds(slot, 1), :]
    unscale = peak_rows[...].T / LEVELS
    square = jnp.zeros((ROWS, COLS), F32)
    for number in range(GROUP):
        value = proj[number].astype(jnp.int32).astype(F32) * unscale[:, number : number + 1]
        unit[:, number * COLS : (number + 1) * COLS] = value
        square = square + value * value
    inv_i = 1.0 / jnp.sqrt(jnp.sum(square, axis=1, keepdims=True) + EPS)
    for number in range(GROUP):
        columns = slice(number * COLS, (number + 1) * COLS)
        value = unit[:, columns] * inv_i
        unit[:, columns] = value
        embs[REACH, :, columns] = value.astype(BF16)
    emb_to_cells()

    def window_terms(left_emb, blocks):
        weights, inners = [], []
        for number in range(WINDOW):
            inner = dot(left_emb, blocks[number], ((1,), (1,)))
            logits = scale * inner + bias
            matched = own_ids == ids_of(number - REACH)
            gradient = softplus_parts(logits)[1] - matched.astype(F32)
            weights.append((scale * gradient).astype(BF16))
            inners.append(inner)
        return jnp.concatenate(weights, axis=1), inners

    def window_totals(inners):
        totals = [jnp.zeros((1, COLS), F32) for _ in range(3)]
        for number, inner in enumerate(inners):
            logits = scale * inner + bias
            matched = own_ids == ids_of(number - REACH)
            tail, sigmoid = softplus_parts(logits)
            gradient = sigmoid - matched.astype(F32)
            loss = tail - jnp.minimum(jnp.where(matched, logits, -logits), 0.0)
            for place, term in enumerate((loss, gradient, gradient * inner)):
                totals[place] = totals[place] + jnp.sum(term, axis=0, keepdims=True)
        return totals

    weight, inners = window_terms(embs[REACH], poses)
    grad_img = dot(weight, poses[...].reshape(WINDOW * ROWS, WIDTH), ((1,), (0,)))
    unit_img = unit[...]
    along = jnp.sum(unit_img * grad_img, axis=1, keepdims=True)
    grad_proj = ((grad_img - unit_img * along) * inv_i).astype(BF16)
    for number in range(GROUP):
        gp_src[number] = grad_proj[:, number * COLS : (number + 1) * COLS]
    gp_copies = []
    for step in FAR_FIRST:
        to = mate_slot(step)
        copy = remote(gp_src.at[to], gp.at[slot], gp_s.at[step], gp_r.at[step], base + to)
        copy.start()
        gp_copies.append(copy)
    gp[slot] = gp_src[slot]

    totals = window_totals(inners)
    for place in range(3):
        tot_src[place : place + 1, :] = totals[place]
    tot_copies = []
    for step in FAR_FIRST:
        copy = remote(tot_src, tot_group.at[slot], tot_s.at[step], tot_r.at[step], base + mate_slot(step))
        copy.start()
        tot_copies.append(copy)
    tot_group[slot] = tot_src[...]

    for copy in gp_copies:
        copy.wait_recv()
    emb_direct()
    emb_relay(0)
    for of_y in range(SIDE):
        value = dot(feats_t[of_y * ROWS : (of_y + 1) * ROWS, :], gp[...].reshape(GROUP * ROWS, COLS), ((1,), (0,)))
        part_src[of_y * SIDE : (of_y + 1) * SIDE] = value.astype(BF16).reshape(SIDE, TILE, COLS)
    for down, over in PLANE:
        to = lines[down] + spots[over]
        remote(part_src.at[to], part.at[cell], part_s, part_r, to * GROUP + slot).start()
    part[cell] = part_src[cell]
    emb_relay(1)

    for copy in tot_copies:
        copy.wait_recv()
    group_sum = tot_group[0]
    for number in range(1, GROUP):
        group_sum = group_sum + tot_group[number]
    tot_z_src[...] = group_sum
    tot_z[z] = group_sum
    z_copies = []
    for step in SIDE_FAR_FIRST:
        copy = remote(tot_z_src, tot_z.at[z], tot_s.at[8 + step], tot_r.at[8 + step], at(y, turned(z, step)))
        copy.start()
        z_copies.append(copy)

    emb_forward(0)
    emb_forward(1)
    for copy in z_copies:
        copy.wait_recv()
    z_sum = tot_z[0]
    for number in range(1, SIDE):
        z_sum = z_sum + tot_z[number]
    tot_y_src[...] = z_sum
    tot_y[y] = z_sum
    y_copies = []
    for step in SIDE_FAR_FIRST:
        copy = remote(tot_y_src, tot_y.at[y], tot_s.at[16 + step], tot_r.at[16 + step], at(turned(y, step), z))
        copy.start()
        y_copies.append(copy)

    pltpu.make_async_copy(part.at[pl.ds(0, CELLS - 1)], part.at[pl.ds(0, CELLS - 1)], part_r).wait()

    summed = jnp.sum(part[...].astype(F32), axis=0)
    for number in range(GROUP):
        fin_src[number, 0:2, :] = summed[2 * number : 2 * number + 2, :]
    fin_copies = []
    for step in FAR_FIRST:
        to = mate_slot(step)
        copy = remote(fin_src.at[to], fin.at[slot], fin_s.at[step], fin_r.at[step], base + to)
        copy.start()
        fin_copies.append(copy)
    fin[slot] = fin_src[slot]

    emb_finish()
    pose_weight, _ = window_terms(poses[REACH], embs)
    grad_pose = dot(pose_weight, embs[...].reshape(WINDOW * ROWS, WIDTH), ((1,), (0,)))
    inv_q = inv_pose[:, 0:1]
    unit_pose = pose_raw[...].astype(F32) * inv_q
    along_pose = jnp.sum(unit_pose * grad_pose, axis=1, keepdims=True)
    pose_out[...] = ((grad_pose - unit_pose * along_pose) * inv_q).astype(BF16)
    store_pose = pltpu.make_async_copy(pose_out, pose_grad_hbm, local_sem.at[4])
    store_pose.start()

    for copy in y_copies:
        copy.wait_recv()
    y_sum = tot_y[0]
    for number in range(1, SIDE):
        y_sum = y_sum + tot_y[number]
    y_sum = y_sum / BATCH
    loss_ref[0] = jnp.sum(y_sum[0:1, :])
    loss_ref[1] = jnp.sum(y_sum[1:2, :])
    scale_grad_ref[0] = jnp.sum(y_sum[2:3, :])

    store_pose.wait()
    for copy in piece_copies + proj_copies + gp_copies:
        copy.wait_send()
    for copy in tot_copies + z_copies + y_copies:
        copy.wait_send()
    for copy in (right_a, left_b, right_b, left_a, right_a2, left_b2, block_own, block_left, block_right, block_far):
        copy.wait_send()
    pose_drain()
    emb_drain()
    pltpu.make_async_copy(head.at[pl.ds(0, CELLS - 1)], head.at[pl.ds(0, CELLS - 1)], head_s).wait()
    pltpu.make_async_copy(part_src.at[pl.ds(0, CELLS - 1)], part_src.at[pl.ds(0, CELLS - 1)], part_s).wait()

    for copy in fin_copies:
        copy.wait()
    for number in range(GROUP):
        head_grad_ref[:, number * COLS : (number + 1) * COLS] = fin[number, 0:2, :]


def local(features, head_rows, poses, match_ids, logit_scale, logit_bias):
    vmem = pl.BlockSpec(memory_space=pltpu.VMEM)
    smem = pl.BlockSpec(memory_space=pltpu.SMEM)
    hbm = pl.BlockSpec(memory_space=pltpu.HBM)
    dma = pltpu.SemaphoreType.DMA
    block = (ROWS, WIDTH)
    square = (GROUP, ROWS, COLS)
    shapes = (
        jax.ShapeDtypeStruct(block, BF16),
        jax.ShapeDtypeStruct((2, WIDTH), F32),
        jax.ShapeDtypeStruct((2,), F32),
        jax.ShapeDtypeStruct((1,), F32),
    )
    return pl.pallas_call(
        kernel,
        name="contrastive",
        out_shape=shapes,
        in_specs=[hbm, hbm, hbm, hbm, vmem, vmem],
        out_specs=(hbm, vmem, smem, smem),
        scratch_shapes=[
            pltpu.VMEM((GROUP,) + block, BF16),
            pltpu.VMEM((WIDTH, GROUP * ROWS), BF16),
            pltpu.VMEM(block, BF16),
            pltpu.VMEM((WINDOW,) + block, BF16),
            pltpu.VMEM((WINDOW,) + block, BF16),
            pltpu.VMEM(block, BF16),
            pltpu.VMEM(block, BF16),
            pltpu.VMEM(block, BF16),
            pltpu.VMEM((COUNT, ROWS), jnp.int32),
            pltpu.VMEM((2, WIDTH), BF16),
            pltpu.VMEM((GROUP, 8, COLS), F32),
            pltpu.VMEM((GROUP, 8, COLS), F32),
            pltpu.VMEM((TILE, COLS), F32),
            pltpu.VMEM((CELLS, TILE, COLS), BF16),
            pltpu.VMEM(square, jnp.int16),
            pltpu.VMEM(square, jnp.int16),
            pltpu.VMEM((GROUP, COLS), F32),
            pltpu.VMEM((GROUP, GROUP, COLS), F32),
            pltpu.VMEM((ROWS, COLS), F32),
            pltpu.VMEM(block, F32),
            pltpu.VMEM((ROWS, COLS), F32),
            pltpu.VMEM(square, BF16),
            pltpu.VMEM(square, BF16),
            pltpu.VMEM((CELLS, TILE, COLS), BF16),
            pltpu.VMEM((CELLS, TILE, COLS), BF16),
            pltpu.VMEM((GROUP, 8, COLS), F32),
            pltpu.VMEM((GROUP, 8, COLS), F32),
            pltpu.VMEM((8, COLS), F32),
            pltpu.VMEM((GROUP, 8, COLS), F32),
            pltpu.VMEM((8, COLS), F32),
            pltpu.VMEM((SIDE, 8, COLS), F32),
            pltpu.VMEM((8, COLS), F32),
            pltpu.VMEM((SIDE, 8, COLS), F32),
            dma((5,)),
            dma((GROUP,)), dma((GROUP,)),
            dma((10,)), dma((10,)),
            dma, dma,
            dma((2 * WINDOW,)), dma((2 * WINDOW,)),
            dma((2 * WINDOW,)), dma((2 * WINDOW,)),
            dma((2 * GROUP,)), dma((2 * GROUP,)),
            dma((GROUP,)), dma((GROUP,)),
            dma, dma,
            dma((GROUP,)), dma((GROUP,)),
            dma((24,)), dma((24,)),
        ],
        compiler_params=pltpu.CompilerParams(
            collective_id=0, has_side_effects=True, vmem_limit_bytes=53 * 1024 * 1024 + 512 * 1024
        ),
    )(features, head_rows, poses, match_ids.reshape(COUNT, ROWS), logit_scale.reshape(1, 1), logit_bias.reshape(1, 1))


def solution(mesh):
    return jax.shard_map(
        local,
        mesh=mesh,
        in_specs=(P("dp", None), P("dp", None), P("dp", None), P(), P(), P()),
        out_specs=(P("dp", None), P("dp", None), P(), P()),
        check_vma=False,
    )
```

```python
import jax
import jax.numpy as jnp
from jax import lax
from jax.experimental import pallas as pl
from jax.experimental.pallas import tpu as pltpu
from jax.sharding import PartitionSpec as P

REACH = 2
WINDOW = 2 * REACH + 1
EPS = 1e-06
ROWS = 128
COLS = 128
GROUP = 8
SIDE = 8
CELLS = SIDE * SIDE
COUNT = GROUP * CELLS
BATCH = ROWS * COUNT
WIDTH = GROUP * COLS
TILE = 16
HALF = ROWS // 2
LEVELS = 32767.0
SMALLEST = 1e-33
FAR_FIRST = (4, 5, 3, 2, 6, 7, 1)
SIDE_FAR_FIRST = (4, 3, 5, 2, 6, 1, 7)
PLANE = [(down, over) for down in SIDE_FAR_FIRST + (0,) for over in SIDE_FAR_FIRST + (0,) if down or over]

F32 = jnp.float32
BF16 = jnp.bfloat16


def remote(src, dst, send_sem, recv_sem, device):
    return pltpu.make_async_remote_copy(
        src_ref=src,
        dst_ref=dst,
        send_sem=send_sem,
        recv_sem=recv_sem,
        device_id=(device,),
        device_id_type=pl.DeviceIdType.MESH,
    )


def dot(left, right, dims):
    return lax.dot_general(left, right, (dims, ((), ())), preferred_element_type=F32)


def softplus_parts(logits):
    tail = jnp.exp(-jnp.abs(logits))
    share = 1.0 / (1.0 + tail)
    sigmoid = jnp.where(logits >= 0, share, tail * share)
    return jnp.log1p(tail), sigmoid


def kernel(
    feat_hbm, head_hbm, pose_hbm, ids_hbm, scale_ref, bias_ref,
    pose_grad_ref, head_grad_ref, loss_ref, scale_grad_ref,
    feats, feats_t, pose_raw, poses, embs, pose_held, emb_held, ids, head_rows, piece_src, piece, tile_f32, head,
    proj_src, proj, peak_src, peaks, peak_rows, unit, inv_pose, gp_src, gp, part_src, part, fin_src, fin,
    tot_src, tot_group, tot_z_src, tot_z, tot_y_src, tot_y,
    local_sem, piece_s, piece_r, feat_s, feat_r, head_s, head_r, pose_s, pose_r, emb_s, emb_r,
    proj_s, proj_r, gp_s, gp_r, part_s, part_r, fin_s, fin_r, tot_s, tot_r,
):
    me = lax.axis_index("dp")
    slot = lax.rem(me, GROUP)
    cell = me // GROUP
    y = cell // SIDE
    z = lax.rem(cell, SIDE)
    core = lax.rem(me, 2)
    base = me - slot
    sibling = me + 1 - 2 * core
    lines = [lax.rem(y + step, SIDE) * SIDE for step in range(SIDE)]
    spots = [lax.rem(z + step, SIDE) for step in range(SIDE)]

    def mate_slot(step):
        return lax.rem(slot + step, GROUP)

    def turned(place, step):
        return lax.rem(place + step, SIDE)

    def at(of_y, of_z):
        return (of_y * SIDE + of_z) * GROUP + slot

    def ring(step):
        return lax.rem(me + step + COUNT, COUNT)

    loads = [
        pltpu.make_async_copy(source, target, local_sem.at[number])
        for number, (source, target) in enumerate((
            (head_hbm, head_rows),
            (feat_hbm, feats.at[slot]),
            (pose_hbm, pose_raw),
            (ids_hbm, ids),
        ))
    ]
    load_head, load_feat, load_pose, load_ids = loads
    for load in loads:
        load.start()

    barrier = pltpu.get_barrier_semaphore()

    def greet(device):
        pl.semaphore_signal(barrier, inc=1, device_id=(device,), device_id_type=pl.DeviceIdType.MESH)

    for step in FAR_FIRST:
        greet(base + mate_slot(step))
    for down, over in PLANE:
        greet((lines[down] + spots[over]) * GROUP + slot)

    peak_rows[...] = jnp.zeros_like(peak_rows)
    load_head.wait()
    rows = head_rows[...].astype(F32)
    piece_src[...] = jnp.zeros_like(piece_src)
    for number in range(GROUP):
        piece_src[number, 0:2, :] = rows[:, number * COLS : (number + 1) * COLS]
    piece[slot] = piece_src[slot]

    pl.semaphore_wait(barrier, GROUP - 1 + CELLS - 1)

    def exchange(blocks, held, sems, semr):
        def part_of(place, number):
            return blocks.at[place, pl.ds(number * HALF, HALF), :]

        def pair(make):
            return [make(number) for number in range(2)]

        def held_part(number):
            return held.at[pl.ds(number * HALF, HALF), :]

        last = GROUP - 2
        ahead = pair(lambda n: remote(part_of(REACH, n), part_of(0, n), sems.at[n], semr.at[n], ring(2)))
        behind = pair(lambda n: remote(part_of(REACH, n), part_of(4, n), sems.at[2 + n], semr.at[8 + n], ring(-2)))
        ahead_cell = pair(lambda n: remote(part_of(REACH, n), held_part(n), sems.at[n], semr.at[4 + n], ring(GROUP)))
        behind_cell = pair(
            lambda n: remote(part_of(REACH, n), held_part(n), sems.at[2 + n], semr.at[4 + n], ring(-GROUP))
        )
        ahead_relay = pair(lambda n: remote(held_part(n), part_of(0, n), sems.at[8 + n], semr.at[n], base + core))
        behind_relay = pair(
            lambda n: remote(held_part(n), part_of(4, n), sems.at[8 + n], semr.at[8 + n], base + last + core)
        )
        to_own = 1 + 2 * core
        to_pass = 3 - 2 * core
        beside = pair(
            lambda n: remote(part_of(REACH, n), part_of(to_own, n), sems.at[4 + n], semr.at[2 * to_own + n], sibling)
        )
        far = 4 - 4 * core
        passed = pair(
            lambda n: remote(part_of(far, n), part_of(to_pass, n), sems.at[6 + n], semr.at[2 * to_pass + n], sibling)
        )

        def arrived(place, number):
            remote(part_of(REACH, number), part_of(place, number), sems.at[0], semr.at[2 * place + number], sibling).wait_recv()

        def to_cells():
            for number in range(2):
                pl.when(slot >= last)(ahead_cell[number].start)
                pl.when(slot < 2)(behind_cell[number].start)

        def direct():
            for number in range(2):
                pl.when(slot < last)(ahead[number].start)
                pl.when(slot >= 2)(behind[number].start)
            for number in range(2):
                beside[number].start()

        def relay(number):
            @pl.when(slot >= last)
            def _():
                ahead_cell[number].wait_recv()
                ahead_relay[number].start()

            @pl.when(slot < 2)
            def _():
                behind_cell[number].wait_recv()
                behind_relay[number].start()

        def forward(number):
            arrived(far, number)
            passed[number].start()

        def finish():
            for number in range(2):
                for place in (4 * core, 1, 3):
                    arrived(place, number)

        def drain():
            for number in range(2):
                for copies in (ahead, behind, beside, passed):
                    copies[number].wait_send()
                pl.when(slot >= last)(ahead_relay[number].wait_send)
                pl.when(slot < 2)(behind_relay[number].wait_send)

        return to_cells, direct, relay, forward, finish, drain

    pose_to_cells, pose_direct, pose_relay, pose_forward, pose_finish, pose_drain = exchange(
        poses, pose_held, pose_s, pose_r
    )
    emb_to_cells, emb_direct, emb_relay, emb_forward, emb_finish, emb_drain = exchange(embs, emb_held, emb_s, emb_r)

    piece_copies = []
    for step in FAR_FIRST:
        to = mate_slot(step)
        copy = remote(piece_src.at[to], piece.at[slot], piece_s.at[step], piece_r.at[step], base + to)
        copy.start()
        piece_copies.append(copy)

    load_feat.wait()
    right = base + mate_slot(2)
    left = base + mate_slot(6)

    def half(of_slot, number):
        return feats.at[of_slot, pl.ds(number * HALF, HALF), :]

    def send_half(of_slot, number, device, sem):
        copy = remote(half(of_slot, number), half(of_slot, number), feat_s.at[sem], feat_r.at[sem], device)
        copy.start()
        return copy

    def send_block(of_slot, sem):
        copy = remote(feats.at[of_slot], feats.at[of_slot], feat_s.at[sem], feat_r.at[sem], sibling)
        copy.start()
        return copy

    right_a = send_half(slot, 0, right, 0)
    left_b = send_half(slot, 1, left, 1)
    right_b = send_half(slot, 1, right, 2)
    left_a = send_half(slot, 0, left, 3)
    block_own = send_block(slot, 6)

    load_pose.wait()
    raw = pose_raw[...].astype(F32)
    inv_p = 1.0 / jnp.sqrt(jnp.sum(raw * raw, axis=1, keepdims=True) + EPS)
    inv_pose[...] = jnp.broadcast_to(inv_p, (ROWS, COLS))
    poses[REACH] = (raw * inv_p).astype(BF16)
    pose_to_cells()

    for copy in piece_copies:
        copy.wait_recv()
    for number in range(GROUP):
        tile_f32[2 * number : 2 * number + 2, :] = piece[number, 0:2, :]
    head[cell] = tile_f32[...].astype(BF16)
    for down, over in PLANE:
        device = (lines[down] + spots[over]) * GROUP + slot
        remote(head.at[cell], head.at[cell], head_s, head_r, device).start()

    right_a.wait_recv()
    right_a2 = send_half(mate_slot(6), 0, right, 4)
    left_b.wait_recv()
    left_b2 = send_half(mate_slot(2), 1, left, 5)

    pose_direct()
    pose_relay(0)
    pose_relay(1)

    right_b.wait_recv()
    block_left = send_block(mate_slot(6), 7)
    left_a.wait_recv()
    block_right = send_block(mate_slot(2), 8)
    right_a2.wait_recv()
    left_b2.wait_recv()
    block_far = send_block(mate_slot(4), 9)

    pltpu.make_async_copy(head.at[pl.ds(0, CELLS - 1)], head.at[pl.ds(0, CELLS - 1)], head_r).wait()
    for copy in (block_own, block_left, block_right, block_far):
        copy.wait_recv()
    lane = lax.broadcasted_iota(jnp.int32, (ROWS, COLS), 1)
    peak_columns = jnp.zeros((ROWS, COLS), F32)
    proj_copies = []
    for step in FAR_FIRST + (0,):
        to = mate_slot(step)
        value = dot(feats[to], head[...].reshape(WIDTH, COLS), ((1,), (0,)))
        peak = jnp.maximum(jnp.max(jnp.abs(value), axis=1, keepdims=True), SMALLEST)
        coded = jnp.round(value * (LEVELS / peak)).astype(jnp.int32).astype(jnp.int16)
        peak_columns = jnp.where(lane == to, peak, peak_columns)
        if step:
            proj_src[step] = coded
            copy = remote(proj_src.at[step], proj.at[slot], proj_s.at[step], proj_r.at[step], base + to)
            copy.start()
            proj_copies.append(copy)
        else:
            proj[slot] = coded
    peak_src[...] = peak_columns.T[0:GROUP, :]
    peaks[slot] = peak_src[...]
    for step in FAR_FIRST:
        copy = remote(
            peak_src, peaks.at[slot], proj_s.at[GROUP + step], proj_r.at[GROUP + step], base + mate_slot(step)
        )
        copy.start()
        proj_copies.append(copy)

    pose_forward(0)
    pose_forward(1)
    for number in range(GROUP):
        feats_t[:, number * ROWS : (number + 1) * ROWS] = feats[number].T
    load_ids.wait()
    scale = jnp.broadcast_to(scale_ref[...], (ROWS, ROWS))
    bias = jnp.broadcast_to(bias_ref[...], (ROWS, ROWS))

    def ids_of(step):
        return ids[pl.ds(ring(step), 1), :]

    own_ids = jnp.broadcast_to(ids_of(0), (ROWS, ROWS)).T
    tot_src[...] = jnp.zeros_like(tot_src)
    fin_src[...] = jnp.zeros_like(fin_src)
    pose_finish()
    for copy in proj_copies:
        copy.wait_recv()

    for number in range(GROUP):
        peak_rows[number : number + 1, :] = peaks[number, pl.ds(slot, 1), :]
    unscale = peak_rows[...].T / LEVELS
    square = jnp.zeros((ROWS, COLS), F32)
    for number in range(GROUP):
        value = proj[number].astype(jnp.int32).astype(F32) * unscale[:, number : number + 1]
        unit[:, number * COLS : (number + 1) * COLS] = value
        square = square + value * value
    inv_i = 1.0 / jnp.sqrt(jnp.sum(square, axis=1, keepdims=True) + EPS)
    for number in range(GROUP):
        columns = slice(number * COLS, (number + 1) * COLS)
        value = unit[:, columns] * inv_i
        unit[:, columns] = value
        embs[REACH, :, columns] = value.astype(BF16)
    emb_to_cells()

    def window_terms(left_emb, blocks):
        weights, inners = [], []
        for number in range(WINDOW):
            inner = dot(left_emb, blocks[number], ((1,), (1,)))
            logits = scale * inner + bias
            matched = own_ids == ids_of(number - REACH)
            gradient = softplus_parts(logits)[1] - matched.astype(F32)
            weights.append((scale * gradient).astype(BF16))
            inners.append(inner)
        return jnp.concatenate(weights, axis=1), inners

    def window_totals(inners):
        totals = [jnp.zeros((1, COLS), F32) for _ in range(3)]
        for number, inner in enumerate(inners):
            logits = scale * inner + bias
            matched = own_ids == ids_of(number - REACH)
            tail, sigmoid = softplus_parts(logits)
            gradient = sigmoid - matched.astype(F32)
            loss = tail - jnp.minimum(jnp.where(matched, logits, -logits), 0.0)
            for place, term in enumerate((loss, gradient, gradient * inner)):
                totals[place] = totals[place] + jnp.sum(term, axis=0, keepdims=True)
        return totals

    weight, inners = window_terms(embs[REACH], poses)
    grad_img = dot(weight, poses[...].reshape(WINDOW * ROWS, WIDTH), ((1,), (0,)))
    unit_img = unit[...]
    along = jnp.sum(unit_img * grad_img, axis=1, keepdims=True)
    grad_proj = ((grad_img - unit_img * along) * inv_i).astype(BF16)
    for number in range(GROUP):
        gp_src[number] = grad_proj[:, number * COLS : (number + 1) * COLS]
    gp_copies = []
    for step in FAR_FIRST:
        to = mate_slot(step)
        copy = remote(gp_src.at[to], gp.at[slot], gp_s.at[step], gp_r.at[step], base + to)
        copy.start()
        gp_copies.append(copy)
    gp[slot] = gp_src[slot]

    totals = window_totals(inners)
    for place in range(3):
        tot_src[place : place + 1, :] = totals[place]
    tot_copies = []
    for step in FAR_FIRST:
        copy = remote(tot_src, tot_group.at[slot], tot_s.at[step], tot_r.at[step], base + mate_slot(step))
        copy.start()
        tot_copies.append(copy)
    tot_group[slot] = tot_src[...]

    for copy in gp_copies:
        copy.wait_recv()
    emb_direct()
    emb_relay(0)
    for of_y in range(SIDE):
        value = dot(feats_t[of_y * ROWS : (of_y + 1) * ROWS, :], gp[...].reshape(GROUP * ROWS, COLS), ((1,), (0,)))
        part_src[of_y * SIDE : (of_y + 1) * SIDE] = value.astype(BF16).reshape(SIDE, TILE, COLS)
    for down, over in PLANE:
        to = lines[down] + spots[over]
        remote(part_src.at[to], part.at[cell], part_s, part_r, to * GROUP + slot).start()
    part[cell] = part_src[cell]
    emb_relay(1)

    for copy in tot_copies:
        copy.wait_recv()
    group_sum = tot_group[0]
    for number in range(1, GROUP):
        group_sum = group_sum + tot_group[number]
    tot_z_src[...] = group_sum
    tot_z[z] = group_sum
    z_copies = []
    for step in SIDE_FAR_FIRST:
        copy = remote(tot_z_src, tot_z.at[z], tot_s.at[8 + step], tot_r.at[8 + step], at(y, turned(z, step)))
        copy.start()
        z_copies.append(copy)

    emb_forward(0)
    emb_forward(1)
    for copy in z_copies:
        copy.wait_recv()
    z_sum = tot_z[0]
    for number in range(1, SIDE):
        z_sum = z_sum + tot_z[number]
    tot_y_src[...] = z_sum
    tot_y[y] = z_sum
    y_copies = []
    for step in SIDE_FAR_FIRST:
        copy = remote(tot_y_src, tot_y.at[y], tot_s.at[16 + step], tot_r.at[16 + step], at(turned(y, step), z))
        copy.start()
        y_copies.append(copy)

    pltpu.make_async_copy(part.at[pl.ds(0, CELLS - 1)], part.at[pl.ds(0, CELLS - 1)], part_r).wait()

    summed = jnp.sum(part[...].astype(F32), axis=0)
    for number in range(GROUP):
        fin_src[number, 0:2, :] = summed[2 * number : 2 * number + 2, :]
    fin_copies = []
    for step in FAR_FIRST:
        to = mate_slot(step)
        copy = remote(fin_src.at[to], fin.at[slot], fin_s.at[step], fin_r.at[step], base + to)
        copy.start()
        fin_copies.append(copy)
    fin[slot] = fin_src[slot]

    emb_finish()
    pose_weight, _ = window_terms(poses[REACH], embs)
    grad_pose = dot(pose_weight, embs[...].reshape(WINDOW * ROWS, WIDTH), ((1,), (0,)))
    inv_q = inv_pose[:, 0:1]
    unit_pose = pose_raw[...].astype(F32) * inv_q
    along_pose = jnp.sum(unit_pose * grad_pose, axis=1, keepdims=True)
    pose_grad_ref[...] = ((grad_pose - unit_pose * along_pose) * inv_q).astype(BF16)

    for copy in y_copies:
        copy.wait_recv()
    y_sum = tot_y[0]
    for number in range(1, SIDE):
        y_sum = y_sum + tot_y[number]
    y_sum = y_sum / BATCH
    loss_ref[0] = jnp.sum(y_sum[0:1, :])
    loss_ref[1] = jnp.sum(y_sum[1:2, :])
    scale_grad_ref[0] = jnp.sum(y_sum[2:3, :])

    for copy in piece_copies + proj_copies + gp_copies:
        copy.wait_send()
    for copy in tot_copies + z_copies + y_copies:
        copy.wait_send()
    for copy in (right_a, left_b, right_b, left_a, right_a2, left_b2, block_own, block_left, block_right, block_far):
        copy.wait_send()
    pose_drain()
    emb_drain()
    pltpu.make_async_copy(head.at[pl.ds(0, CELLS - 1)], head.at[pl.ds(0, CELLS - 1)], head_s).wait()
    pltpu.make_async_copy(part_src.at[pl.ds(0, CELLS - 1)], part_src.at[pl.ds(0, CELLS - 1)], part_s).wait()

    for copy in fin_copies:
        copy.wait()
    for number in range(GROUP):
        head_grad_ref[:, number * COLS : (number + 1) * COLS] = fin[number, 0:2, :]


def local(features, head_rows, poses, match_ids, logit_scale, logit_bias):
    vmem = pl.BlockSpec(memory_space=pltpu.VMEM)
    smem = pl.BlockSpec(memory_space=pltpu.SMEM)
    hbm = pl.BlockSpec(memory_space=pltpu.HBM)
    dma = pltpu.SemaphoreType.DMA
    block = (ROWS, WIDTH)
    square = (GROUP, ROWS, COLS)
    shapes = (
        jax.ShapeDtypeStruct(block, BF16),
        jax.ShapeDtypeStruct((2, WIDTH), F32),
        jax.ShapeDtypeStruct((2,), F32),
        jax.ShapeDtypeStruct((1,), F32),
    )
    return pl.pallas_call(
        kernel,
        name="contrastive",
        out_shape=shapes,
        in_specs=[hbm, hbm, hbm, hbm, vmem, vmem],
        out_specs=(vmem, vmem, smem, smem),
        scratch_shapes=[
            pltpu.VMEM((GROUP,) + block, BF16),
            pltpu.VMEM((WIDTH, GROUP * ROWS), BF16),
            pltpu.VMEM(block, BF16),
            pltpu.VMEM((WINDOW,) + block, BF16),
            pltpu.VMEM((WINDOW,) + block, BF16),
            pltpu.VMEM(block, BF16),
            pltpu.VMEM(block, BF16),
            pltpu.VMEM((COUNT, ROWS), jnp.int32),
            pltpu.VMEM((2, WIDTH), BF16),
            pltpu.VMEM((GROUP, 8, COLS), F32),
            pltpu.VMEM((GROUP, 8, COLS), F32),
            pltpu.VMEM((TILE, COLS), F32),
            pltpu.VMEM((CELLS, TILE, COLS), BF16),
            pltpu.VMEM(square, jnp.int16),
            pltpu.VMEM(square, jnp.int16),
            pltpu.VMEM((GROUP, COLS), F32),
            pltpu.VMEM((GROUP, GROUP, COLS), F32),
            pltpu.VMEM((ROWS, COLS), F32),
            pltpu.VMEM(block, F32),
            pltpu.VMEM((ROWS, COLS), F32),
            pltpu.VMEM(square, BF16),
            pltpu.VMEM(square, BF16),
            pltpu.VMEM((CELLS, TILE, COLS), BF16),
            pltpu.VMEM((CELLS, TILE, COLS), BF16),
            pltpu.VMEM((GROUP, 8, COLS), F32),
            pltpu.VMEM((GROUP, 8, COLS), F32),
            pltpu.VMEM((8, COLS), F32),
            pltpu.VMEM((GROUP, 8, COLS), F32),
            pltpu.VMEM((8, COLS), F32),
            pltpu.VMEM((SIDE, 8, COLS), F32),
            pltpu.VMEM((8, COLS), F32),
            pltpu.VMEM((SIDE, 8, COLS), F32),
            dma((4,)),
            dma((GROUP,)), dma((GROUP,)),
            dma((10,)), dma((10,)),
            dma, dma,
            dma((2 * WINDOW,)), dma((2 * WINDOW,)),
            dma((2 * WINDOW,)), dma((2 * WINDOW,)),
            dma((2 * GROUP,)), dma((2 * GROUP,)),
            dma((GROUP,)), dma((GROUP,)),
            dma, dma,
            dma((GROUP,)), dma((GROUP,)),
            dma((24,)), dma((24,)),
        ],
        compiler_params=pltpu.CompilerParams(
            collective_id=0, has_side_effects=True, vmem_limit_bytes=53 * 1024 * 1024 + 512 * 1024
        ),
    )(features, head_rows, poses, match_ids.reshape(COUNT, ROWS), logit_scale.reshape(1, 1), logit_bias.reshape(1, 1))


def solution(mesh):
    return jax.shard_map(
        local,
        mesh=mesh,
        in_specs=(P("dp", None), P("dp", None), P("dp", None), P(), P(), P()),
        out_specs=(P("dp", None), P("dp", None), P(), P()),
        check_vma=False,
    )
```
